256 devices in a mesh: img: 64 (over z, y, core), tok: 4 (over x).
Axes of the slice: x: 4, y: 4, z: 8, core: 2. Of those that a mesh axis runs over, the one named last changes fastest.
Arguments:
- tokens: bfloat16 [2048, 128, 1024], P('img', 'tok'), may hold values from -6 to 6
- embed: bfloat16 [1024, 768], replicated, may hold values from -0.1875 to 0.1875
- norm_gain: float32 [768], replicated, may hold values from 0.1 to 1.9
- pairs: int32 [2048, 2], P('img'), may hold values from 0 to 2047, as said below
- wq_first: bfloat16 [768, 768], replicated, may hold values from -0.21875 to 0.21875
- wkv_first: bfloat16 [768, 1536], replicated, may hold values from -0.21875 to 0.21875
- wq_second: bfloat16 [768, 768], replicated, may hold values from -0.21875 to 0.21875
- wkv_second: bfloat16 [768, 1536], replicated, may hold values from -0.21875 to 0.21875
Outputs:
- joined: bfloat16 [2048, 128, 768], P('img', 'tok')
The draws below stay inside these ranges and needn't reach their ends.
Inputs may be any that keep to these rules, and one draw needn't show every extreme that they name: `pairs`: the first image of every row lies among the 32 images owned by the img index that holds the row (images are owned in contiguous runs of 32); the two images of a row differ; among the rows of one img index at most 2 second images share an owner, and exactly 2 do for one owner on every index.
All inputs are finite; a program needn't handle non-finite values.
Results may differ from the reference program's by a relative error of at most 0.0051.
Values may be sent and summed in bfloat16 or wider, within the bound.
No kernel may reach another device: no remote copies, remote signals or barrier semaphores. Data moves between devices by JAX's collectives and lax.ppermute only.
A program may use at most 128 MiB of HBM per device.

```python
import jax
import jax.numpy as jnp
from jax import lax

D = 768
DENC = 1024
HEADS = 12
TOK_IMG = 128
IMG_DEV = 32
PAIR_DEV = 32
IMAGES = 2048


def draw_pairs(key, part):
    key = jax.random.fold_in(key, 11)
    owner_count = IMAGES // IMG_DEV
    capacity = PAIR_DEV // owner_count + 2

    def one_device(device):
        subkey = jax.random.fold_in(key, device)
        keys = jax.random.split(subkey, 5)
        order = jax.random.permutation(keys[0], owner_count)
        places = jnp.arange(PAIR_DEV)
        picked = jnp.where(places < capacity, 0, 1 + (places - capacity) % (owner_count - 1))
        owner_seq = jax.random.permutation(keys[1], order[picked])
        first_local = jax.random.randint(keys[2], (PAIR_DEV,), 0, IMG_DEV)
        other_local = jax.random.randint(keys[3], (PAIR_DEV,), 0, IMG_DEV)
        offset = jax.random.randint(keys[4], (PAIR_DEV,), 1, IMG_DEV)
        second_local = jnp.where(owner_seq == device, (first_local + offset) % IMG_DEV, other_local)
        return jnp.stack([device * IMG_DEV + first_local, owner_seq * IMG_DEV + second_local], axis=1)
    result = jax.vmap(one_device)(jnp.arange(owner_count))
    return result.reshape(owner_count * PAIR_DEV, 2).astype(jnp.int32)


def shard_levels(rng, dims, shards, smallest, high):
    gain, own = 1.0, jax.random.fold_in(rng, 6)
    for dim, parts in shards:
        heights = jnp.exp(jax.random.uniform(jax.random.fold_in(own, dim), (parts,), jnp.float32, smallest / len(shards), high / len(shards)))
        gain = gain * jnp.repeat(heights, dims[dim] // parts).reshape([-1 if axis == dim else 1 for axis in range(len(dims))])
    return gain


def bell_draw(stream_key, shape, scale, most, pieces=(), kind=jnp.bfloat16):
    values = scale * jax.random.normal(stream_key, shape, jnp.float32)
    if pieces:
        values = values * shard_levels(stream_key, shape, pieces, -0.22, 0.18)
    return jnp.clip(values, -most, most).astype(kind)


def setup_inputs(seed: int = 0) -> dict:
    key_of = jax.random.split(jax.random.key(seed), 9)
    tokens = bell_draw(key_of[0], (IMAGES, TOK_IMG, DENC), 1.0, 6.0, ((0, 64), (1, 4)))
    embed = bell_draw(key_of[1], (DENC, D), DENC ** -0.5, 0.1875)
    norm_gain = jnp.clip(1.0 + 0.18 * jax.random.normal(key_of[2], (D,), jnp.float32), 0.1, 1.9)
    pairs = draw_pairs(jax.random.fold_in(key_of[8], 71), 0)
    wq_first = bell_draw(key_of[4], (D, D), D ** -0.5, 0.21875)
    wkv_first = bell_draw(key_of[5], (D, 2 * D), D ** -0.5, 0.21875)
    wq_second = bell_draw(key_of[6], (D, D), D ** -0.5, 0.21875)
    wkv_second = bell_draw(key_of[7], (D, 2 * D), D ** -0.5, 0.21875)
    return dict(tokens=tokens, embed=embed, norm_gain=norm_gain, pairs=pairs, wq_first=wq_first, wkv_first=wkv_first, wq_second=wq_second, wkv_second=wkv_second)


def layer_norm(values, norm_gain):
    centred = values - lax.optimization_barrier(jnp.mean(values, axis=-1, keepdims=True))
    spread = lax.optimization_barrier(jnp.mean(centred * centred, axis=-1, keepdims=True))
    return centred * lax.rsqrt(spread + 1e-06) * norm_gain

def project(inputs, weight):
    flat = inputs.reshape(-1, inputs.shape[-1])
    result = jnp.dot(flat, weight, preferred_element_type=jnp.float32).astype(jnp.bfloat16)
    return result.reshape(inputs.shape[0], inputs.shape[1], weight.shape[1])

def attend(queries, keyvals, head_count):
    batch, rows, width = queries.shape
    head_size = width // head_count
    keys = keyvals[:, :, :width].astype(jnp.float32).reshape(batch, -1, head_count, head_size)
    values = keyvals[:, :, width:].astype(jnp.float32).reshape(batch, -1, head_count, head_size)
    query_heads = queries.astype(jnp.float32).reshape(batch, rows, head_count, head_size)
    scores = jnp.einsum('pqhe,pkhe->phqk', query_heads, keys) * (1.0 / math_sqrt(head_size))
    scores = scores - lax.optimization_barrier(jnp.max(scores, axis=-1, keepdims=True))
    expd = jnp.exp(scores)
    weights = (expd / lax.optimization_barrier(jnp.sum(expd, axis=-1, keepdims=True))).astype(jnp.bfloat16)
    output = jnp.einsum('phqk,pkhe->pqhe', weights.astype(jnp.float32), values)
    return output.reshape(batch, rows, width).astype(jnp.bfloat16)

def math_sqrt(number):
    return float(number) ** 0.5

def reference(tokens, embed, norm_gain, pairs, wq_first, wkv_first, wq_second, wkv_second):
    width = embed.shape[1]
    embedded = jnp.dot(tokens.reshape(IMAGES * TOK_IMG, DENC), embed, preferred_element_type=jnp.float32)
    normed = layer_norm(embedded, norm_gain).astype(jnp.bfloat16).reshape(IMAGES, TOK_IMG, width)
    blocks = pairs.reshape(IMAGES // IMG_DEV, PAIR_DEV, 2)

    def visit(total, block):
        first_img = normed[block[:, 0]]
        second_img = normed[block[:, 1]]
        cross_first = attend(project(first_img, wq_first), project(second_img, wkv_first), HEADS)
        cross_second = attend(project(second_img, wq_second), project(first_img, wkv_second), HEADS)
        total = total.at[block[:, 0]].add(cross_first.astype(jnp.float32))
        total = total.at[block[:, 1]].add(cross_second.astype(jnp.float32))
        return (total, None)
    total, _ = lax.scan(visit, jnp.zeros((IMAGES, TOK_IMG, width), jnp.float32), blocks)
    count = jnp.zeros((IMAGES,), jnp.float32).at[pairs.reshape(-1)].add(1.0)
    joined = total / jnp.maximum(count, 1.0)[:, None, None] + normed.astype(jnp.float32)
    return joined.astype(jnp.bfloat16)
```

```python
import functools

import jax
import jax.numpy as jnp
from jax import lax
from jax.experimental import pallas as pl
from jax.experimental.pallas import tpu as pltpu
from jax.sharding import PartitionSpec as P

HEAD = 64
VMEM_LIMIT = 56 * 1024 * 1024
F32 = jnp.float32
BF16 = jnp.bfloat16


def call(kernel, out_shape, flops, nbytes, **kwargs):
    return pl.pallas_call(
        kernel,
        out_shape=out_shape,
        compiler_params=pltpu.CompilerParams(vmem_limit_bytes=VMEM_LIMIT),
        cost_estimate=pl.CostEstimate(flops=flops, bytes_accessed=nbytes, transcendentals=0),
        **kwargs,
    )


def whole(*shape):
    return pl.BlockSpec(shape, lambda *_: (0,) * len(shape))


def embed_kernel(first_ref, tok_ref, x_ref, w_ref, gain_ref, normed_ref, pieces_ref, f0, f1, f2, f3, scratch):
    step = pl.program_id(0)
    rows = x_ref.shape[0]
    width = w_ref.shape[1]
    half = width // 2
    e = jnp.dot(x_ref[...], w_ref[...], preferred_element_type=F32)
    c = e - jnp.mean(e, axis=-1, keepdims=True)
    spread = jnp.mean(c * c, axis=-1, keepdims=True)
    n = c * lax.rsqrt(spread + 1e-06) * gain_ref[...]
    normed_ref[...] = n.astype(BF16)
    lane_blocks = width // 128
    start = pl.multiple_of(step * rows, rows)
    for b in range(lane_blocks):
        scratch[b, pl.ds(start, rows), :] = n[:, b * 128:(b + 1) * 128]

    @pl.when(step == pl.num_programs(0) - 1)
    def _():
        images = pieces_ref.shape[1]
        toks = scratch.shape[1] // images
        for r in range(toks):
            for b in range(lane_blocks):
                v = scratch[b, pl.ds(r, images, stride=toks), :].astype(BF16)
                h, at = divmod(b * 128, half)
                pieces_ref[h * toks + r, :, at:at + 128] = v
        group = tok_ref[0]
        for k, f in enumerate((f0, f1, f2, f3)):
            items = f.shape[0]
            for j in range(items):
                p = first_ref[lax.rem(group + k, 4) * items + j]
                at = pl.multiple_of(p * toks, toks)
                for b in range(lane_blocks):
                    f[j, :, b * 128:(b + 1) * 128] = scratch[b, pl.ds(at, toks), :].astype(BF16)


def pick_kernel(ids_ref, table_ref, out_ref):
    rows = ids_ref.shape[0]
    count = table_ref.shape[0]
    ids = ids_ref[...]
    lane = lax.broadcasted_iota(jnp.int32, (rows, 128), 1)
    hot = [(ids - b * 128 == lane).astype(F32).astype(BF16) for b in range(count // 128)]
    hot = jnp.concatenate(hot, axis=1)
    out_ref[...] = jnp.dot(hot, table_ref[...], preferred_element_type=F32).astype(BF16)


def sum_kernel(ids_ref, rows_ref, out_ref):
    step = pl.program_id(0)
    images = out_ref.shape[0]
    image = lax.broadcasted_iota(jnp.int32, (images, ids_ref.shape[1]), 0) + step * images
    hot = (ids_ref[...] == image).astype(F32).astype(BF16)
    out_ref[...] = jnp.dot(hot, rows_ref[...], preferred_element_type=F32).astype(BF16)


def first_kernel(f0, f1, f2, f3, wq_ref, wkv_ref, q_ref, kv_ref):
    for k, f in enumerate((f0, f1, f2, f3)):
        items, toks, width = f.shape
        x = f[...].reshape(items * toks, width)
        q = jnp.dot(x, wq_ref[...], preferred_element_type=F32).astype(BF16)
        q_ref[:, k * toks:(k + 1) * toks, :] = q.reshape(items, toks, -1)
        kv = jnp.dot(x, wkv_ref[...], preferred_element_type=F32).astype(BF16)
        kv_ref[:, k * toks:(k + 1) * toks, :] = kv.reshape(items, toks, -1)


def masks(rows):
    lane = lax.broadcasted_iota(jnp.int32, (rows, 128), 1)
    low = lane < HEAD
    one_low = jnp.where(low, 1.0, 0.0).astype(BF16)
    one_high = jnp.where(low, 0.0, 1.0).astype(BF16)
    return low, one_low, one_high


def attend(q, k, v, low, one_low, one_high):
    rows = k.shape[0]
    zero = jnp.zeros((rows, 128), BF16)
    kk = jnp.concatenate([jnp.where(low, k, zero), jnp.where(low, zero, k)], axis=0)
    top = jnp.concatenate([jnp.where(low, v, zero), one_low], axis=1)
    bottom = jnp.concatenate([jnp.where(low, zero, v), one_high], axis=1)
    vv = jnp.concatenate([top, bottom], axis=0)
    s = lax.dot_general(q, kk, (((1,), (1,)), ((), ())), preferred_element_type=F32)
    s = s * (1.0 / HEAD ** 0.5)
    parts = []
    for part in (s[:, :rows], s[:, rows:]):
        parts.append(jnp.exp(part - jnp.max(part, axis=-1, keepdims=True)).astype(BF16))
    o = jnp.dot(jnp.concatenate(parts, axis=1), vv, preferred_element_type=F32)
    return o[:, :128] / o[:, 128:]


def decode_kernel(x_ref, q_ref, kv_ref, wq_ref, wkv_ref, g0, g1, g2, g3, back_ref, scratch, o_scr, x_scr, q_scr, kv_scr):
    step = pl.program_id(0)
    steps = pl.num_programs(0)
    lane_blocks = scratch.shape[0]
    per_half = lane_blocks // 2
    rows = scratch.shape[1]
    toks = q_ref.shape[1]

    @pl.when(step == 0)
    def _():
        for b in range(lane_blocks):
            h, at = divmod(b, per_half)
            scratch[b] = x_ref[h, :, at * 128:(at + 1) * 128].astype(F32)
        items = rows // toks
        for j in range(items):
            for b in range(lane_blocks):
                x_scr[j * toks:(j + 1) * toks, b * 128:(b + 1) * 128] = scratch[
                    b, pl.ds(j, toks, stride=items), :
                ].astype(BF16)

        @pl.loop(0, rows // 256)
        def _(i):
            at = pl.ds(pl.multiple_of(i * 256, 256), 256)
            x = x_scr[at, :]
            q_scr[at, :] = jnp.dot(x, wq_ref[...], preferred_element_type=F32).astype(BF16)
            kv_scr[at, :] = jnp.dot(x, wkv_ref[...], preferred_element_type=F32).astype(BF16)

    mine = pl.ds(pl.multiple_of(step * toks, toks), toks)

    width = lane_blocks * 128
    part = toks // 4
    masked = masks(toks)

    @pl.loop(0, lane_blocks // 2)
    def _(i):
        for u in range(2):
            h = i * 2 + u
            lo = pl.multiple_of(h * 128, 128)
            keys = pl.ds(lo, 128)
            values = pl.ds(pl.multiple_of(lo + width, 128), 128)
            o = attend(q_ref[0, :, keys], kv_scr[mine, keys], kv_scr[mine, values], *masked).astype(BF16)
            for k, g in enumerate((g0, g1, g2, g3)):
                g[0, :, keys] = o[k * part:(k + 1) * part]
            o_scr[h, mine, :] = attend(q_scr[mine, keys], kv_ref[0, :, keys], kv_ref[0, :, values], *masked)

    @pl.when(step == steps - 1)
    def _():
        for b in range(lane_blocks):
            h, at = divmod(b, per_half)
            for j in range(rows // toks):
                scratch[b, pl.ds(j, toks, stride=rows // toks), :] = o_scr[b, j * toks:(j + 1) * toks, :]
            back_ref[h, :, at * 128:(at + 1) * 128] = scratch[b].astype(BF16)


def near_kernel(first_ref, tok_ref, r0, r1, r2, r3, acc_ref):
    acc_ref[...] = jnp.zeros_like(acc_ref)
    group = tok_ref[0]
    for k, r in enumerate((r0, r1, r2, r3)):
        items = r.shape[0]

        @pl.loop(0, items)
        def _(j, r=r, k=k, items=items):
            p = first_ref[lax.rem(group + k, 4) * items + j]
            acc_ref[p] = acc_ref[p] + r[j].astype(F32)


def join_kernel(recip_ref, far_ref, acc_ref, normed_ref, out_ref, scratch):
    images, toks, width = acc_ref.shape
    half = width // 2
    lane_blocks = width // 128
    for r in range(toks):
        for b in range(lane_blocks):
            h, at = divmod(b * 128, half)
            scratch[b, pl.ds(r, images, stride=toks), :] = far_ref[h * toks + r, :, at:at + 128].astype(F32)

    @pl.loop(0, images)
    def _(i):
        recip = recip_ref[i]
        at = pl.ds(pl.multiple_of(i * toks, toks), toks)
        for b in range(lane_blocks):
            lanes = slice(b * 128, (b + 1) * 128)
            total = scratch[b, at, :] + acc_ref[i, :, lanes]
            out_ref[i, :, lanes] = (total * recip + normed_ref[at, lanes].astype(F32)).astype(BF16)


def body(tokens, embed, norm_gain, pairs, wq_first, wkv_first, wq_second, wkv_second):
    images, toks, enc = tokens.shape
    width = embed.shape[1]
    half = width // 2
    owners = lax.axis_size("img")
    groups = lax.axis_size("tok")
    count = pairs.shape[0]
    items = count // groups
    total = owners * count
    all_images = owners * images
    rows = images * toks
    img = lax.axis_index("img")
    tok = lax.axis_index("tok").astype(jnp.int32).reshape(1)
    smem = pl.BlockSpec(memory_space=pltpu.SMEM)
    vmem = pl.BlockSpec(memory_space=pltpu.VMEM)

    first_local = pairs[:, 0] - img * images
    all_pairs = lax.all_gather(pairs, "img", axis=0, tiled=True)
    second = all_pairs[:, 1]
    own_ids = img * images + jnp.arange(images)
    seen = jnp.sum((all_pairs.reshape(1, -1) == own_ids[:, None]).astype(F32), axis=1)
    recip = 1.0 / jnp.maximum(seen, 1.0)

    part = jax.ShapeDtypeStruct((items, toks, width), BF16)
    block = 256
    normed, pieces, f0, f1, f2, f3 = call(
        embed_kernel,
        [
            jax.ShapeDtypeStruct((rows, width), BF16),
            jax.ShapeDtypeStruct((owners, images, half), BF16),
            part, part, part, part,
        ],
        2 * rows * enc * width,
        2 * rows * (enc + 3 * width) + 2 * enc * width,
        grid=(rows // block,),
        in_specs=[
            smem, smem,
            pl.BlockSpec((block, enc), lambda i: (i, 0)),
            whole(enc, width),
            whole(1, width),
        ],
        out_specs=[
            pl.BlockSpec((block, width), lambda i: (i, 0)),
            whole(owners, images, half),
        ] + [whole(items, toks, width)] * 4,
        scratch_shapes=[pltpu.VMEM((width // 128, rows, 128), F32)],
        name="embed",
    )(first_local, tok, tokens.reshape(rows, enc), embed, norm_gain.reshape(1, width))

    table = lax.all_to_all(pieces, "img", split_axis=0, concat_axis=0, tiled=True)
    firsts = [f0]
    for k, f in enumerate((f1, f2, f3)):
        perm = [(t, (t + k + 1) % groups) for t in range(groups)]
        firsts.append(lax.ppermute(f, "tok", perm))

    step_rows = 256
    ids = jnp.broadcast_to(second[:, None], (total, 128))
    asked = call(
        pick_kernel,
        jax.ShapeDtypeStruct((total, half), BF16),
        2 * total * all_images * half,
        2 * (total + all_images) * half,
        grid=(total // step_rows,),
        in_specs=[
            pl.BlockSpec((step_rows, 128), lambda i: (i, 0)),
            whole(all_images, half),
        ],
        out_specs=pl.BlockSpec((step_rows, half), lambda i: (i, 0)),
        name="pick",
    )(ids, table.reshape(all_images, half))
    seconds = lax.all_to_all(
        asked.reshape(owners * groups, items, half), ("img", "tok"), split_axis=0, concat_axis=0, tiled=True
    )

    whole_toks = toks * groups
    q_first, kv_second = call(
        first_kernel,
        [
            jax.ShapeDtypeStruct((items, whole_toks, width), BF16),
            jax.ShapeDtypeStruct((items, whole_toks, 2 * width), BF16),
        ],
        2 * items * whole_toks * width * 3 * width,
        2 * items * whole_toks * width * 4 + 6 * width * width,
        in_specs=[vmem] * 6,
        out_specs=[vmem] * 2,
        name="first",
    )(*firsts, wq_first, wkv_second)

    pair_rows = items * whole_toks
    g0, g1, g2, g3, back = call(
        decode_kernel,
        [part, part, part, part, jax.ShapeDtypeStruct((2, pair_rows, half), BF16)],
        2 * pair_rows * width * 3 * width + 16 * pair_rows * whole_toks * width,
        2 * pair_rows * width * 6 + 6 * width * width,
        grid=(items,),
        in_specs=[
            whole(2, pair_rows, half),
            pl.BlockSpec((1, whole_toks, width), lambda j: (j, 0, 0)),
            pl.BlockSpec((1, whole_toks, 2 * width), lambda j: (j, 0, 0)),
            whole(width, width),
            whole(width, 2 * width),
        ],
        out_specs=[pl.BlockSpec((1, toks, width), lambda j: (j, 0, 0))] * 4 + [whole(2, pair_rows, half)],
        scratch_shapes=[
            pltpu.VMEM((width // 128, pair_rows, 128), F32),
            pltpu.VMEM((width // 128, pair_rows, 128), F32),
            pltpu.VMEM((pair_rows, width), BF16),
            pltpu.VMEM((pair_rows, width), BF16),
            pltpu.VMEM((pair_rows, 2 * width), BF16),
        ],
        name="decode",
    )(seconds.reshape(2, pair_rows, half), q_first, kv_second, wq_second, wkv_first)

    returned = lax.all_to_all(
        back.reshape(owners * groups, items, half), ("img", "tok"), split_axis=0, concat_axis=0, tiled=True
    )
    near = [g0]
    for k, g in enumerate((g1, g2, g3)):
        perm = [(t, (t - k - 1) % groups) for t in range(groups)]
        near.append(lax.ppermute(g, "tok", perm))
    acc = call(
        near_kernel,
        jax.ShapeDtypeStruct((images, toks, width), F32),
        rows * width,
        6 * rows * width,
        in_specs=[smem, smem] + [vmem] * 4,
        out_specs=vmem,
        name="near",
    )(first_local, tok, *near)
    sums = call(
        sum_kernel,
        jax.ShapeDtypeStruct((all_images, half), BF16),
        2 * total * all_images * half,
        2 * (total + all_images) * half,
        grid=(all_images // step_rows,),
        in_specs=[whole(1, total), whole(total, half)],
        out_specs=pl.BlockSpec((step_rows, half), lambda i: (i, 0)),
        name="sum",
    )(second.reshape(1, total), returned.reshape(total, half))
    far = lax.all_to_all(
        sums.reshape(owners, images, half), "img", split_axis=0, concat_axis=0, tiled=True
    )
    return call(
        join_kernel,
        jax.ShapeDtypeStruct((images, toks, width), BF16),
        rows * width * 4,
        rows * width * 10,
        in_specs=[smem] + [vmem] * 3,
        out_specs=vmem,
        scratch_shapes=[pltpu.VMEM((width // 128, rows, 128), F32)],
        name="join",
    )(recip, far, acc, normed)


def solution(mesh):
    in_specs = (P("img", "tok", None), P(), P(), P("img", None), P(), P(), P(), P())
    out_specs = P("img", "tok", None)
    return jax.shard_map(body, mesh=mesh, in_specs=in_specs, out_specs=out_specs, check_vma=False)
```

```python
import jax
import jax.numpy as jnp
from jax import lax
from jax.experimental import pallas as pl
from jax.experimental.pallas import tpu as pltpu
from jax.sharding import PartitionSpec as P

HEAD = 64
MIB = 1024 * 1024
F32 = jnp.float32
BF16 = jnp.bfloat16


def call(kernel, out_shape, flops, nbytes, vmem_mib, **kwargs):
    return pl.pallas_call(
        kernel,
        out_shape=out_shape,
        compiler_params=pltpu.CompilerParams(vmem_limit_bytes=vmem_mib * MIB),
        cost_estimate=pl.CostEstimate(flops=flops, bytes_accessed=nbytes, transcendentals=0),
        **kwargs,
    )


def hbm(x):
    return pltpu.with_memory_space_constraint(x, pltpu.HBM)


def whole(*shape):
    return pl.BlockSpec(shape, lambda *_: (0,) * len(shape))


def embed_kernel(x_ref, w_ref, gain_ref, ids_ref, normed_ref, pieces_ref, scratch):
    step = pl.program_id(0)
    rows = x_ref.shape[0]
    width = w_ref.shape[1]
    e = jnp.dot(x_ref[...], w_ref[...], preferred_element_type=F32)
    c = e - jnp.mean(e, axis=-1, keepdims=True)
    spread = jnp.mean(c * c, axis=-1, keepdims=True)
    n = c * lax.rsqrt(spread + 1e-06) * gain_ref[...]
    normed_ref[...] = n.astype(BF16)
    start = pl.multiple_of(step * rows, rows)
    for b in range(width // 128):
        scratch[b, pl.ds(start, rows), :] = n[:, b * 128:(b + 1) * 128]

    @pl.when(step == pl.num_programs(0) - 1)
    def _():
        per_half = width // 256
        toks = pieces_ref.shape[0] // 2
        images = scratch.shape[1] // toks
        for r in range(toks):
            for b in range(width // 128):
                h, at = divmod(b, per_half)
                v = scratch[b, pl.ds(r, images, stride=toks), :]
                pieces_ref[h * toks + r, at * images:(at + 1) * images, :] = v.astype(BF16)
        for m in range(2 * toks):
            pieces_ref[m, per_half * images:, :] = ids_ref[...]


def gather_kernel(first_ref, tok_ref, normed_ref, f0, f1, f2, f3):
    group = tok_ref[0]
    for k, f in enumerate((f0, f1, f2, f3)):
        items, toks, _ = f.shape
        for j in range(items):
            p = first_ref[lax.rem(group + k, 4) * items + j]
            f[j] = normed_ref[pl.ds(pl.multiple_of(p * toks, toks), toks), :]


def pick_kernel(table_ref, out_ref, ids_ref):
    step = pl.program_id(0)
    owners, height, _ = table_ref.shape
    rows, half = out_ref.shape
    blocks = half // 128
    images = (height - 8) // blocks
    lane = lax.broadcasted_iota(jnp.int32, (images, 128), 1)
    diagonal = lane == lax.broadcasted_iota(jnp.int32, (images, 128), 0)
    per_step = rows // images
    wanted = []
    for o in range(per_step):
        top = table_ref[step * per_step + o, blocks * images:, :].astype(F32)
        number = top[0:1, :] * float(images) + top[1:2, :]
        ids_ref[o] = number
        column = jnp.sum(jnp.where(diagonal, number, 0.0), axis=1, keepdims=True)
        wanted.append(jnp.broadcast_to(column, (images, 128)))
    wanted = jnp.concatenate(wanted, axis=0)
    lane = lax.broadcasted_iota(jnp.int32, (rows, 128), 1).astype(F32)
    hot = [jnp.where(wanted == lane + float(b * 128), 1.0, 0.0).astype(BF16) for b in range(owners * images // 128)]
    hot = jnp.concatenate(hot, axis=1)
    table = [table_ref[:, b * images:(b + 1) * images, :].reshape(owners * images, 128) for b in range(blocks)]
    out_ref[...] = jnp.dot(hot, jnp.concatenate(table, axis=1), preferred_element_type=F32).astype(BF16)


def sum_kernel(ids_ref, rows_ref, out_ref):
    step = pl.program_id(0)
    images = out_ref.shape[0]
    image = lax.broadcasted_iota(jnp.int32, (images, ids_ref.shape[1]), 0) + step * images
    hot = jnp.where(ids_ref[...] == image, 1.0, 0.0).astype(BF16)
    out_ref[...] = jnp.dot(hot, rows_ref[...], preferred_element_type=F32).astype(BF16)


def first_kernel(f0, f1, f2, f3, wq_ref, wkv_ref, q_ref, kv_ref):
    for k, f in enumerate((f0, f1, f2, f3)):
        items, toks, width = f.shape
        x = f[...].reshape(items * toks, width)
        q = jnp.dot(x, wq_ref[...], preferred_element_type=F32).astype(BF16)
        q_ref[:, k * toks:(k + 1) * toks, :] = q.reshape(items, toks, -1)
        kv = jnp.dot(x, wkv_ref[...], preferred_element_type=F32).astype(BF16)
        kv_ref[:, k * toks:(k + 1) * toks, :] = kv.reshape(items, toks, -1)


def masks(rows):
    lane = lax.broadcasted_iota(jnp.int32, (rows, 128), 1)
    low = lane < HEAD
    one_low = jnp.where(low, 1.0, 0.0).astype(BF16)
    one_high = jnp.where(low, 0.0, 1.0).astype(BF16)
    return low, one_low, one_high


def attend(q, k, v, low, one_low, one_high):
    rows = k.shape[0]
    zero = jnp.zeros((rows, 128), BF16)
    kk = jnp.concatenate([jnp.where(low, k, zero), jnp.where(low, zero, k)], axis=0)
    top = jnp.concatenate([jnp.where(low, v, zero), one_low], axis=1)
    bottom = jnp.concatenate([jnp.where(low, zero, v), one_high], axis=1)
    vv = jnp.concatenate([top, bottom], axis=0)
    s = lax.dot_general(q, kk, (((1,), (1,)), ((), ())), preferred_element_type=F32)
    s = s * (1.0 / HEAD ** 0.5)
    parts = []
    for part in (s[:, :rows], s[:, rows:]):
        parts.append(jnp.exp(part - jnp.max(part, axis=-1, keepdims=True)).astype(BF16))
    o = jnp.dot(jnp.concatenate(parts, axis=1), vv, preferred_element_type=F32)
    return o[:, :128] / o[:, 128:]


def by_pair(x_ref, scratch, x_scr, items):
    per_half = scratch.shape[0] // 2
    toks = scratch.shape[1] // items
    for b in range(scratch.shape[0]):
        h, at = divmod(b, per_half)
        scratch[b] = x_ref[h, :, at * 128:(at + 1) * 128].astype(F32)
        for j in range(items):
            rows = scratch[b, pl.ds(j, toks, stride=items), :]
            x_scr[j * toks:(j + 1) * toks, b * 128:(b + 1) * 128] = rows.astype(BF16)


def second_kernel(x_ref, kv_ref, wq_ref, back_ref, scratch, o_scr, x_scr, q_scr):
    step = pl.program_id(0)
    lane_blocks = scratch.shape[0]
    per_half = lane_blocks // 2
    rows = scratch.shape[1]
    toks = kv_ref.shape[1]
    width = lane_blocks * 128
    items = rows // toks

    @pl.when(step == 0)
    def _():
        by_pair(x_ref, scratch, x_scr, items)

        for i in range(rows // 256):
            at = slice(i * 256, (i + 1) * 256)
            q_scr[at, :] = jnp.dot(x_scr[at, :], wq_ref[...], preferred_element_type=F32).astype(BF16)

    mine = pl.ds(pl.multiple_of(step * toks, toks), toks)
    masked = masks(toks)
    for h in range(lane_blocks):
        at = slice(h * 128, (h + 1) * 128)
        k = kv_ref[0, :, at]
        v = kv_ref[0, :, width + h * 128:width + (h + 1) * 128]
        o_scr[h, mine, :] = attend(q_scr[mine, at], k, v, *masked)

    @pl.when(step == pl.num_programs(0) - 1)
    def _():
        for b in range(lane_blocks):
            h, at = divmod(b, per_half)
            for j in range(items):
                scratch[b, pl.ds(j, toks, stride=items), :] = o_scr[b, j * toks:(j + 1) * toks, :]
            back_ref[h, :, at * 128:(at + 1) * 128] = scratch[b].astype(BF16)


def near_kernel(x_ref, q_ref, wkv_ref, g0, g1, g2, g3, scratch, x_scr, kv_scr):
    step = pl.program_id(0)
    lane_blocks = scratch.shape[0]
    rows = scratch.shape[1]
    toks = q_ref.shape[1]
    width = lane_blocks * 128

    @pl.when(step == 0)
    def _():
        by_pair(x_ref, scratch, x_scr, rows // toks)

        @pl.loop(0, rows // 256)
        def _(i):
            at = pl.ds(pl.multiple_of(i * 256, 256), 256)
            kv_scr[at, :] = jnp.dot(x_scr[at, :], wkv_ref[...], preferred_element_type=F32).astype(BF16)

    mine = pl.ds(pl.multiple_of(step * toks, toks), toks)
    masked = masks(toks)
    part = toks // 4
    for h in range(lane_blocks):
        at = slice(h * 128, (h + 1) * 128)
        v = kv_scr[mine, width + h * 128:width + (h + 1) * 128]
        o = attend(q_ref[0, :, at], kv_scr[mine, at], v, *masked).astype(BF16)
        for k, g in enumerate((g0, g1, g2, g3)):
            g[0, :, at] = o[k * part:(k + 1) * part]


def base_kernel(first_ref, tok_ref, recip_ref, normed_ref, r0, r1, r2, r3, out_ref):
    images, toks, _ = out_ref.shape
    out_ref[...] = jnp.zeros_like(out_ref)
    group = tok_ref[0]
    for k, r in enumerate((r0, r1, r2, r3)):
        items = r.shape[0]

        @pl.loop(0, items)
        def _(j, r=r, k=k, items=items):
            p = first_ref[lax.rem(group + k, 4) * items + j]
            out_ref[p] = out_ref[p] + r[j].astype(F32)

    @pl.loop(0, images)
    def _(i):
        at = pl.ds(pl.multiple_of(i * toks, toks), toks)
        out_ref[i] = out_ref[i] * recip_ref[i] + normed_ref[at, :].astype(F32)


def join_kernel(recip_ref, far_ref, base_ref, out_ref, scratch):
    images, toks, width = base_ref.shape
    half = width // 2
    lane_blocks = width // 128
    first = pl.program_id(0) * images
    for b in range(lane_blocks):
        h, at = divmod(b * 128, half)
        for r in range(toks):
            scratch[b, pl.ds(r, images, stride=toks), :] = far_ref[h * toks + r, :, at:at + 128].astype(F32)
    for i in range(images):
        recip = recip_ref[first + i]
        for b in range(lane_blocks):
            lanes = slice(b * 128, (b + 1) * 128)
            far = scratch[b, i * toks:(i + 1) * toks, :]
            out_ref[i, :, lanes] = (far * recip + base_ref[i, :, lanes]).astype(BF16)


def body(tokens, embed, norm_gain, pairs, wq_first, wkv_first, wq_second, wkv_second):
    images, toks, enc = tokens.shape
    width = embed.shape[1]
    half = width // 2
    owners = lax.axis_size("img")
    groups = lax.axis_size("tok")
    count = pairs.shape[0]
    items = count // groups
    total = owners * count
    all_images = owners * images
    rows = images * toks
    img = lax.axis_index("img")
    tok = lax.axis_index("tok").astype(jnp.int32).reshape(1)
    smem = pl.BlockSpec(memory_space=pltpu.SMEM)
    vmem = pl.BlockSpec(memory_space=pltpu.VMEM)

    first_local = pairs[:, 0] - img * images
    part = jax.ShapeDtypeStruct((items, toks, width), BF16)
    second_owner = pairs[:, 1] // images
    numbers = jnp.stack([second_owner, pairs[:, 1] - second_owner * images]).astype(BF16)
    numbers = jnp.pad(numbers, ((0, 6), (0, 128 - count)))
    block = 256
    height = images * half // 128 + 8
    normed, pieces = call(
        embed_kernel,
        [
            pltpu.HBM((rows, width), BF16),
            pltpu.HBM((owners, height, 128), BF16),
        ],
        2 * rows * enc * width,
        2 * rows * (enc + 2 * width) + 2 * enc * width,
        28,
        grid=(rows // block,),
        in_specs=[
            pl.BlockSpec((block, enc), lambda i: (i, 0)),
            whole(enc, width),
            whole(1, width),
            whole(8, 128),
        ],
        out_specs=[
            pl.BlockSpec((block, width), lambda i: (i, 0)),
            whole(owners, height, 128),
        ],
        scratch_shapes=[pltpu.VMEM((width // 128, rows, 128), F32)],
        name="embed",
    )(hbm(tokens.reshape(rows, enc)), hbm(embed), norm_gain.reshape(1, width), numbers)

    table = lax.all_to_all(pieces, "img", split_axis=0, concat_axis=0, tiled=True)

    firsts = list(call(
        gather_kernel,
        [part] * 4,
        rows * width,
        4 * rows * width,
        8,
        in_specs=[smem, smem, vmem],
        out_specs=[vmem] * 4,
        name="gather",
    )(first_local, tok, normed))
    for k in range(1, groups):
        perm = [(t, (t + k) % groups) for t in range(groups)]
        firsts[k] = lax.ppermute(firsts[k], "tok", perm)
    table, *firsts = lax.optimization_barrier((table, *firsts))

    step_rows = 512
    asked, ids = call(
        pick_kernel,
        [
            pltpu.HBM((total, half), BF16),
            jax.ShapeDtypeStruct((owners, 1, 128), F32),
        ],
        2 * total * all_images * half,
        2 * (total + all_images) * half,
        16,
        grid=(total // step_rows,),
        in_specs=[whole(owners, height, 128)],
        out_specs=[
            pl.BlockSpec((step_rows, half), lambda i: (i, 0)),
            pl.BlockSpec((step_rows // count, 1, 128), lambda i: (i, 0, 0)),
        ],
        name="pick",
    )(table)
    ids = ids[:, 0, :count].astype(jnp.int32).reshape(total)
    seconds = lax.all_to_all(
        asked.reshape(owners * groups, items, half), ("img", "tok"), split_axis=0, concat_axis=0, tiled=True
    )

    whole_toks = toks * groups
    pair_rows = items * whole_toks
    q_first, kv_second = call(
        first_kernel,
        [
            jax.ShapeDtypeStruct((items, whole_toks, width), BF16),
            jax.ShapeDtypeStruct((items, whole_toks, 2 * width), BF16),
        ],
        2 * pair_rows * width * 3 * width,
        2 * pair_rows * width * 4 + 6 * width * width,
        20,
        in_specs=[vmem] * 6,
        out_specs=[vmem] * 2,
        name="first",
    )(*firsts, wq_first, wkv_second)
    own_ids = img * images + jnp.arange(images)
    seen = jnp.sum((ids[None, :] == own_ids[:, None]).astype(F32), axis=1)
    seen = seen + jnp.sum((pairs[:, 0][None, :] == own_ids[:, None]).astype(F32), axis=1)
    recip = 1.0 / jnp.maximum(seen, 1.0)

    seconds = seconds.reshape(2, pair_rows, half)
    back = call(
        second_kernel,
        pltpu.HBM((2, pair_rows, half), BF16),
        2 * pair_rows * width * width + 8 * pair_rows * whole_toks * width,
        2 * pair_rows * width * 4 + 2 * width * width,
        28,
        grid=(items,),
        in_specs=[
            whole(2, pair_rows, half),
            pl.BlockSpec((1, whole_toks, 2 * width), lambda j: (j, 0, 0)),
            whole(width, width),
        ],
        out_specs=whole(2, pair_rows, half),
        scratch_shapes=[
            pltpu.VMEM((width // 128, pair_rows, 128), F32),
            pltpu.VMEM((width // 128, pair_rows, 128), F32),
            pltpu.VMEM((pair_rows, width), BF16),
            pltpu.VMEM((pair_rows, width), BF16),
        ],
        name="second",
    )(seconds, kv_second, wq_second)
    returned = lax.all_to_all(
        back.reshape(owners * groups, items, half), ("img", "tok"), split_axis=0, concat_axis=0, tiled=True
    )

    seconds, _ = lax.optimization_barrier((seconds, back))
    near = list(call(
        near_kernel,
        [part] * 4,
        4 * pair_rows * width * width + 8 * pair_rows * whole_toks * width,
        2 * pair_rows * width * 3 + 4 * width * width,
        28,
        grid=(items,),
        in_specs=[
            whole(2, pair_rows, half),
            pl.BlockSpec((1, whole_toks, width), lambda j: (j, 0, 0)),
            whole(width, 2 * width),
        ],
        out_specs=[pl.BlockSpec((1, toks, width), lambda j: (j, 0, 0))] * 4,
        scratch_shapes=[
            pltpu.VMEM((width // 128, pair_rows, 128), F32),
            pltpu.VMEM((pair_rows, width), BF16),
            pltpu.VMEM((pair_rows, 2 * width), BF16),
        ],
        name="near",
    )(seconds, q_first, wkv_first))
    returned, *near = lax.optimization_barrier((returned, *near))
    for k in range(1, groups):
        perm = [(t, (t - k) % groups) for t in range(groups)]
        near[k] = lax.ppermute(near[k], "tok", perm)

    sums = call(
        sum_kernel,
        pltpu.HBM((all_images, half), BF16),
        2 * total * all_images * half,
        2 * (total + all_images) * half,
        16,
        grid=(all_images // step_rows,),
        in_specs=[whole(1, total), whole(total, half)],
        out_specs=pl.BlockSpec((step_rows, half), lambda i: (i, 0)),
        name="sum",
    )(ids.reshape(1, total), returned.reshape(total, half))
    far = lax.all_to_all(
        sums.reshape(owners, images, half), "img", split_axis=0, concat_axis=0, tiled=True
    )
    base = call(
        base_kernel,
        jax.ShapeDtypeStruct((images, toks, width), F32),
        rows * width,
        8 * rows * width,
        12,
        in_specs=[smem, smem, smem] + [vmem] * 5,
        out_specs=vmem,
        name="base",
    )(first_local, tok, recip, normed, *near)
    block = images // 2
    return call(
        join_kernel,
        jax.ShapeDtypeStruct((images, toks, width), BF16),
        rows * width * 4,
        rows * width * 8,
        16,
        grid=(images // block,),
        in_specs=[
            smem,
            pl.BlockSpec((owners, block, half), lambda i: (0, i, 0)),
            pl.BlockSpec((block, toks, width), lambda i: (i, 0, 0)),
        ],
        out_specs=pl.BlockSpec((block, toks, width), lambda i: (i, 0, 0)),
        scratch_shapes=[pltpu.VMEM((width // 128, block * toks, 128), F32)],
        name="join",
    )(recip, far, base)


def solution(mesh):
    in_specs = (P("img", "tok", None), P(), P(), P("img", None), P(), P(), P(), P())
    out_specs = P("img", "tok", None)
    return jax.shard_map(body, mesh=mesh, in_specs=in_specs, out_specs=out_specs, check_vma=False)
```

```python
import jax
import jax.numpy as jnp
from jax import lax
from jax.experimental import pallas as pl
from jax.experimental.pallas import tpu as pltpu
from jax.sharding import PartitionSpec as P

HEAD = 64
MIB = 1024 * 1024
F32 = jnp.float32
BF16 = jnp.bfloat16


def call(kernel, out_shape, flops, nbytes, vmem_mib, **kwargs):
    return pl.pallas_call(
        kernel,
        out_shape=out_shape,
        compiler_params=pltpu.CompilerParams(vmem_limit_bytes=vmem_mib * MIB),
        cost_estimate=pl.CostEstimate(flops=flops, bytes_accessed=nbytes, transcendentals=0),
        **kwargs,
    )


def hbm(x):
    return pltpu.with_memory_space_constraint(x, pltpu.HBM)


def whole(*shape):
    return pl.BlockSpec(shape, lambda *_: (0,) * len(shape))


def embed_kernel(
    x_hbm, w_hbm, gain_hbm, pairs_hbm, normed_hbm, pieces_hbm,
    x_scr, w_scr, gain_scr, pairs_scr, normed_scr, pieces_scr, scratch, in_sems, normed_sems, piece_sems,
):
    chunks, rows, _ = x_scr.shape
    width = w_scr.shape[1]
    per_half = width // 256
    toks = pieces_scr.shape[0] // 2
    pitch = toks + 8
    images = scratch.shape[1] // pitch
    small = [
        pltpu.make_async_copy(pairs_hbm, pairs_scr, in_sems.at[chunks + 1]),
        pltpu.make_async_copy(gain_hbm, gain_scr, in_sems.at[chunks + 2]),
    ]
    loads = [pltpu.make_async_copy(w_hbm, w_scr, in_sems.at[chunks])]
    for i in range(chunks):
        loads.append(pltpu.make_async_copy(x_hbm.at[pl.ds(i * rows, rows)], x_scr.at[i], in_sems.at[i]))
    for load in loads + small:
        load.start()
    for load in small:
        load.wait()
    gain = gain_scr[...].reshape(1, width)
    second = pairs_scr[1:2, :]
    owner = lax.div(second, images)
    numbers = jnp.concatenate([owner, second - owner * images], axis=0).astype(F32)
    numbers = jnp.concatenate([numbers, jnp.zeros((6, numbers.shape[1]), F32)], axis=0)
    numbers = jnp.concatenate([numbers, jnp.zeros((8, 128 - numbers.shape[1]), F32)], axis=1).astype(BF16)
    for m in range(2 * toks):
        pieces_scr[m, per_half * images:, :] = numbers
    loads[0].wait()
    stores = []
    for i in range(chunks):
        loads[i + 1].wait()
        at = pl.ds(i * rows, rows)
        e = jnp.dot(x_scr[i], w_scr[...], preferred_element_type=F32)
        c = e - jnp.mean(e, axis=-1, keepdims=True)
        spread = jnp.mean(c * c, axis=-1, keepdims=True)
        n = c * lax.rsqrt(spread + 1e-06) * gain
        normed_scr[at, :] = n.astype(BF16)
        stores.append(pltpu.make_async_copy(normed_scr.at[at], normed_hbm.at[at], normed_sems.at[i]))
        stores[-1].start()
        for u in range(rows // toks):
            to = pl.ds((i * (rows // toks) + u) * pitch, toks)
            for b in range(width // 128):
                scratch[b, to, :] = n[u * toks:(u + 1) * toks, b * 128:(b + 1) * 128]
    group = 8
    for h in range(2):
        for r in range(toks):
            for b in range(per_half):
                v = scratch[h * per_half + b, pl.ds(r, images, stride=pitch), :]
                pieces_scr[h * toks + r, b * images:(b + 1) * images, :] = v.astype(BF16)
            if r % group == group - 1:
                first = h * toks + r - group + 1
                at = pl.ds(first, group)
                sem = piece_sems.at[first // group]
                stores.append(pltpu.make_async_copy(pieces_scr.at[at], pieces_hbm.at[at], sem))
                stores[-1].start()
    for store in stores:
        store.wait()


def gather_kernel(first_ref, tok_ref, normed_ref, f0, f1, f2, f3):
    group = tok_ref[0]
    for k, f in enumerate((f0, f1, f2, f3)):
        items, toks, _ = f.shape
        for j in range(items):
            p = first_ref[lax.rem(group + k, 4) * items + j]
            f[j] = normed_ref[pl.ds(pl.multiple_of(p * toks, toks), toks), :]


def pick_kernel(table_ref, out_ref, ids_ref):
    step = pl.program_id(0)
    owners, height, _ = table_ref.shape
    rows, half = out_ref.shape
    blocks = half // 128
    images = (height - 8) // blocks
    lane = lax.broadcasted_iota(jnp.int32, (images, 128), 1)
    diagonal = lane == lax.broadcasted_iota(jnp.int32, (images, 128), 0)
    per_step = rows // images
    wanted = []
    for o in range(per_step):
        top = table_ref[step * per_step + o, blocks * images:, :].astype(F32)
        number = top[0:1, :] * float(images) + top[1:2, :]
        ids_ref[o] = number
        column = jnp.sum(jnp.where(diagonal, number, 0.0), axis=1, keepdims=True)
        wanted.append(jnp.broadcast_to(column, (images, 128)))
    wanted = jnp.concatenate(wanted, axis=0)
    lane = lax.broadcasted_iota(jnp.int32, (rows, 128), 1).astype(F32)
    hot = [jnp.where(wanted == lane + float(b * 128), 1.0, 0.0).astype(BF16) for b in range(owners * images // 128)]
    hot = jnp.concatenate(hot, axis=1)
    table = [table_ref[:, b * images:(b + 1) * images, :].reshape(owners * images, 128) for b in range(blocks)]
    out_ref[...] = jnp.dot(hot, jnp.concatenate(table, axis=1), preferred_element_type=F32).astype(BF16)


def sum_kernel(ids_ref, rows_ref, out_ref):
    step = pl.program_id(0)
    images = out_ref.shape[0]
    image = lax.broadcasted_iota(jnp.int32, (images, ids_ref.shape[1]), 0) + step * images
    hot = jnp.where(ids_ref[...] == image, 1.0, 0.0).astype(BF16)
    out_ref[...] = jnp.dot(hot, rows_ref[...], preferred_element_type=F32).astype(BF16)


def first_kernel(f0, f1, f2, f3, wq_ref, wkv_ref, q_ref, kv_ref):
    for k, f in enumerate((f0, f1, f2, f3)):
        items, toks, width = f.shape
        x = f[...].reshape(items * toks, width)
        q = jnp.dot(x, wq_ref[...], preferred_element_type=F32).astype(BF16)
        q_ref[:, k * toks:(k + 1) * toks, :] = q.reshape(items, toks, -1)
        kv = jnp.dot(x, wkv_ref[...], preferred_element_type=F32).astype(BF16)
        kv_ref[:, k * toks:(k + 1) * toks, :] = kv.reshape(items, toks, -1)


def masks(rows):
    lane = lax.broadcasted_iota(jnp.int32, (rows, 128), 1)
    low = lane < HEAD
    one_low = jnp.where(low, 1.0, 0.0).astype(BF16)
    one_high = jnp.where(low, 0.0, 1.0).astype(BF16)
    return low, one_low, one_high


def attend(q, k, v, low, one_low, one_high):
    rows = k.shape[0]
    zero = jnp.zeros((rows, 128), BF16)
    kk = jnp.concatenate([jnp.where(low, k, zero), jnp.where(low, zero, k)], axis=0)
    top = jnp.concatenate([jnp.where(low, v, zero), one_low], axis=1)
    bottom = jnp.concatenate([jnp.where(low, zero, v), one_high], axis=1)
    vv = jnp.concatenate([top, bottom], axis=0)
    s = lax.dot_general(q, kk, (((1,), (1,)), ((), ())), preferred_element_type=F32)
    s = s * (1.0 / HEAD ** 0.5)
    parts = []
    for part in (s[:, :rows], s[:, rows:]):
        parts.append(jnp.exp(part - jnp.max(part, axis=-1, keepdims=True)).astype(BF16))
    o = jnp.dot(jnp.concatenate(parts, axis=1), vv, preferred_element_type=F32)
    return o[:, :128] / o[:, 128:]


def by_pair(x_ref, scratch, x_scr, items):
    per_half = scratch.shape[0] // 2
    toks = scratch.shape[1] // items
    for b in range(scratch.shape[0]):
        h, at = divmod(b, per_half)
        scratch[b] = x_ref[h, :, at * 128:(at + 1) * 128].astype(F32)
        for j in range(items):
            rows = scratch[b, pl.ds(j, toks, stride=items), :]
            x_scr[j * toks:(j + 1) * toks, b * 128:(b + 1) * 128] = rows.astype(BF16)


def second_kernel(x_ref, kv_ref, wq_ref, back_ref, q_scr, o_scr):
    step = pl.program_id(0)
    steps = pl.num_programs(0)
    lane_blocks, rows, _ = q_scr.shape
    per_half = lane_blocks // 2
    per_step, toks, _ = kv_ref.shape
    width = lane_blocks * 128
    items = rows // toks

    @pl.when(step == 0)
    def _():
        for i in range(rows // 256):
            at = slice(i * 256, (i + 1) * 256)
            x = jnp.concatenate([x_ref[0, at, :], x_ref[1, at, :]], axis=1)
            q = jnp.dot(x, wq_ref[...], preferred_element_type=F32)
            for b in range(lane_blocks):
                q_scr[b, at, :] = q[:, b * 128:(b + 1) * 128]

    masked = masks(toks)
    for p in range(per_step):
        mine = pl.ds(step * per_step + p, toks, stride=items)
        for h in range(lane_blocks):
            k = kv_ref[p, :, h * 128:(h + 1) * 128]
            v = kv_ref[p, :, width + h * 128:width + (h + 1) * 128]
            o_scr[h, mine, :] = attend(q_scr[h, mine, :].astype(BF16), k, v, *masked)

    @pl.when(step == steps - 1)
    def _():
        for b in range(lane_blocks):
            h, at = divmod(b, per_half)
            back_ref[h, :, at * 128:(at + 1) * 128] = o_scr[b].astype(BF16)


def near_kernel(x_ref, q_ref, wkv_ref, g0, g1, g2, g3, scratch, x_scr, kv_scr):
    step = pl.program_id(0)
    lane_blocks = scratch.shape[0]
    rows = scratch.shape[1]
    toks = q_ref.shape[1]
    width = lane_blocks * 128

    @pl.when(step == 0)
    def _():
        by_pair(x_ref, scratch, x_scr, rows // toks)

        @pl.loop(0, rows // 256)
        def _(i):
            at = pl.ds(pl.multiple_of(i * 256, 256), 256)
            kv_scr[at, :] = jnp.dot(x_scr[at, :], wkv_ref[...], preferred_element_type=F32).astype(BF16)

    mine = pl.ds(pl.multiple_of(step * toks, toks), toks)
    masked = masks(toks)
    part = toks // 4
    for h in range(lane_blocks):
        at = slice(h * 128, (h + 1) * 128)
        v = kv_scr[mine, width + h * 128:width + (h + 1) * 128]
        o = attend(q_ref[0, :, at], kv_scr[mine, at], v, *masked).astype(BF16)
        for k, g in enumerate((g0, g1, g2, g3)):
            g[0, :, at] = o[k * part:(k + 1) * part]


def base_kernel(first_ref, tok_ref, recip_ref, normed_ref, r0, r1, r2, r3, out_ref):
    images, toks, _ = out_ref.shape
    out_ref[...] = jnp.zeros_like(out_ref)
    group = tok_ref[0]
    for k, r in enumerate((r0, r1, r2, r3)):
        items = r.shape[0]

        @pl.loop(0, items)
        def _(j, r=r, k=k, items=items):
            p = first_ref[lax.rem(group + k, 4) * items + j]
            out_ref[p] = out_ref[p] + r[j].astype(F32)

    @pl.loop(0, images)
    def _(i):
        at = pl.ds(pl.multiple_of(i * toks, toks), toks)
        out_ref[i] = out_ref[i] * recip_ref[i] + normed_ref[at, :].astype(F32)


def join_kernel(recip_ref, far_ref, base_ref, out_hbm, out_scr, scratch, sems):
    images, toks, width = base_ref.shape
    half = width // 2
    lane_blocks = width // 128
    pitch = toks + 8
    group = scratch.shape[1] // pitch
    stores = []
    for g in range(images // group):
        for b in range(lane_blocks):
            h, at = divmod(b * 128, half)
            for r in range(toks):
                far = far_ref[h * toks + r, g * group:(g + 1) * group, at:at + 128]
                scratch[b, pl.ds(r, group, stride=pitch), :] = far.astype(F32)
        for u in range(group):
            i = g * group + u
            recip = recip_ref[i]
            for b in range(lane_blocks):
                lanes = slice(b * 128, (b + 1) * 128)
                far = scratch[b, u * pitch:u * pitch + toks, :]
                out_scr[i, :, lanes] = (far * recip + base_ref[i, :, lanes]).astype(BF16)
            if u % 8 == 7:
                at = pl.ds(i - 7, 8)
                stores.append(pltpu.make_async_copy(out_scr.at[at], out_hbm.at[at], sems.at[i // 8]))
                stores[-1].start()
    for store in stores:
        store.wait()


def body(tokens, embed, norm_gain, pairs, wq_first, wkv_first, wq_second, wkv_second):
    images, toks, enc = tokens.shape
    width = embed.shape[1]
    half = width // 2
    owners = lax.axis_size("img")
    groups = lax.axis_size("tok")
    count = pairs.shape[0]
    items = count // groups
    total = owners * count
    all_images = owners * images
    rows = images * toks
    img = lax.axis_index("img")
    tok = lax.axis_index("tok").astype(jnp.int32).reshape(1)
    smem = pl.BlockSpec(memory_space=pltpu.SMEM)
    vmem = pl.BlockSpec(memory_space=pltpu.VMEM)

    first_local = pairs[:, 0] - img * images
    part = jax.ShapeDtypeStruct((items, toks, width), BF16)
    block = 256
    height = images * half // 128 + 8
    anywhere = pl.BlockSpec(memory_space=pl.ANY)
    normed, pieces = call(
        embed_kernel,
        [
            pltpu.HBM((rows, width), BF16),
            pltpu.HBM((owners, height, 128), BF16),
        ],
        2 * rows * enc * width,
        2 * rows * (enc + 2 * width) + 2 * enc * width,
        28,
        in_specs=[anywhere] * 4,
        out_specs=[anywhere, anywhere],
        scratch_shapes=[
            pltpu.VMEM((rows // block, block, enc), BF16),
            pltpu.VMEM((enc, width), BF16),
            pltpu.VMEM((width,), F32),
            pltpu.VMEM((2, count), jnp.int32),
            pltpu.VMEM((rows, width), BF16),
            pltpu.VMEM((owners, height, 128), BF16),
            pltpu.VMEM((width // 128, images * (toks + 8), 128), F32),
            pltpu.SemaphoreType.DMA((rows // block + 3,)),
            pltpu.SemaphoreType.DMA((rows // block,)),
            pltpu.SemaphoreType.DMA((owners // 8,)),
        ],
        name="embed",
    )(hbm(tokens.reshape(rows, enc)), hbm(embed), hbm(norm_gain), hbm(pairs.T))

    table = lax.all_to_all(pieces, "img", split_axis=0, concat_axis=0, tiled=True)

    firsts = list(call(
        gather_kernel,
        [part] * 4,
        rows * width,
        4 * rows * width,
        8,
        in_specs=[smem, smem, vmem],
        out_specs=[vmem] * 4,
        name="gather",
    )(first_local, tok, normed))
    for k in range(1, groups):
        perm = [(t, (t + k) % groups) for t in range(groups)]
        firsts[k] = lax.ppermute(firsts[k], "tok", perm)
    table, *firsts = lax.optimization_barrier((table, *firsts))

    step_rows = 512
    asked, ids = call(
        pick_kernel,
        [
            pltpu.HBM((total, half), BF16),
            jax.ShapeDtypeStruct((owners, 1, 128), F32),
        ],
        2 * total * all_images * half,
        2 * (total + all_images) * half,
        16,
        grid=(total // step_rows,),
        in_specs=[vmem],
        out_specs=[
            pl.BlockSpec((step_rows, half), lambda i: (i, 0)),
            pl.BlockSpec((step_rows // count, 1, 128), lambda i: (i, 0, 0)),
        ],
        name="pick",
    )(table)
    ids = ids[:, 0, :count].astype(jnp.int32).reshape(total)
    seconds = lax.all_to_all(
        asked.reshape(owners * groups, items, half), ("img", "tok"), split_axis=0, concat_axis=0, tiled=True
    )

    whole_toks = toks * groups
    pair_rows = items * whole_toks
    q_first, kv_second = call(
        first_kernel,
        [
            jax.ShapeDtypeStruct((items, whole_toks, width), BF16),
            jax.ShapeDtypeStruct((items, whole_toks, 2 * width), BF16),
        ],
        2 * pair_rows * width * 3 * width,
        2 * pair_rows * width * 4 + 6 * width * width,
        20,
        in_specs=[vmem] * 6,
        out_specs=[vmem] * 2,
        name="first",
    )(*firsts, wq_first, wkv_second)
    own_ids = img * images + jnp.arange(images)
    seen = jnp.sum((ids[None, :] == own_ids[:, None]).astype(F32), axis=1)
    seen = seen + jnp.sum((pairs[:, 0][None, :] == own_ids[:, None]).astype(F32), axis=1)
    recip = 1.0 / jnp.maximum(seen, 1.0)

    seconds = seconds.reshape(2, pair_rows, half)
    back = call(
        second_kernel,
        pltpu.HBM((2, pair_rows, half), BF16),
        2 * pair_rows * width * width + 8 * pair_rows * whole_toks * width,
        2 * pair_rows * width * 4 + 2 * width * width,
        28,
        grid=(items // 2,),
        in_specs=[
            vmem,
            pl.BlockSpec((2, whole_toks, 2 * width), lambda j: (j, 0, 0)),
            vmem,
        ],
        out_specs=whole(2, pair_rows, half),
        scratch_shapes=[
            pltpu.VMEM((width // 128, pair_rows, 128), F32),
            pltpu.VMEM((width // 128, pair_rows, 128), F32),
        ],
        name="second",
    )(seconds, hbm(kv_second), wq_second)
    returned = lax.all_to_all(
        back.reshape(owners * groups, items, half), ("img", "tok"), split_axis=0, concat_axis=0, tiled=True
    )

    seconds, _ = lax.optimization_barrier((seconds, back))
    near = list(call(
        near_kernel,
        [part] * 4,
        4 * pair_rows * width * width + 8 * pair_rows * whole_toks * width,
        2 * pair_rows * width * 3 + 4 * width * width,
        28,
        grid=(items,),
        in_specs=[
            vmem,
            pl.BlockSpec((1, whole_toks, width), lambda j: (j, 0, 0)),
            vmem,
        ],
        out_specs=[pl.BlockSpec((1, toks, width), lambda j: (j, 0, 0))] * 4,
        scratch_shapes=[
            pltpu.VMEM((width // 128, pair_rows, 128), F32),
            pltpu.VMEM((pair_rows, width), BF16),
            pltpu.VMEM((pair_rows, 2 * width), BF16),
        ],
        name="near",
    )(seconds, q_first, wkv_first))
    returned, *near = lax.optimization_barrier((returned, *near))
    for k in range(1, groups):
        perm = [(t, (t - k) % groups) for t in range(groups)]
        near[k] = lax.ppermute(near[k], "tok", perm)

    sums = call(
        sum_kernel,
        pltpu.HBM((all_images, half), BF16),
        2 * total * all_images * half,
        2 * (total + all_images) * half,
        16,
        grid=(all_images // step_rows,),
        in_specs=[vmem, vmem],
        out_specs=pl.BlockSpec((step_rows, half), lambda i: (i, 0)),
        name="sum",
    )(ids.reshape(1, total), returned.reshape(total, half))
    far = lax.all_to_all(
        sums.reshape(owners, images, half), "img", split_axis=0, concat_axis=0, tiled=True
    )
    base = call(
        base_kernel,
        jax.ShapeDtypeStruct((images, toks, width), F32),
        rows * width,
        8 * rows * width,
        12,
        in_specs=[smem, smem, smem] + [vmem] * 5,
        out_specs=vmem,
        name="base",
    )(first_local, tok, recip, normed, *near)
    return call(
        join_kernel,
        pltpu.HBM((images, toks, width), BF16),
        rows * width * 4,
        rows * width * 8,
        24,
        in_specs=[smem, vmem, vmem],
        out_specs=anywhere,
        scratch_shapes=[
            pltpu.VMEM((images, toks, width), BF16),
            pltpu.VMEM((width // 128, images // 2 * (toks + 8), 128), F32),
            pltpu.SemaphoreType.DMA((images // 8,)),
        ],
        name="join",
    )(recip, far, base)


def solution(mesh):
    in_specs = (P("img", "tok", None), P(), P(), P("img", None), P(), P(), P(), P())
    out_specs = P("img", "tok", None)
    return jax.shard_map(body, mesh=mesh, in_specs=in_specs, out_specs=out_specs, check_vma=False)
```

```python
import jax
import jax.numpy as jnp
from jax import lax
from jax.experimental import pallas as pl
from jax.experimental.pallas import tpu as pltpu
from jax.sharding import PartitionSpec as P

HEAD = 64
MIB = 1024 * 1024
F32 = jnp.float32
BF16 = jnp.bfloat16


def call(kernel, out_shape, flops, nbytes, vmem_mib, **kwargs):
    return pl.pallas_call(
        kernel,
        out_shape=out_shape,
        compiler_params=pltpu.CompilerParams(vmem_limit_bytes=vmem_mib * MIB),
        cost_estimate=pl.CostEstimate(flops=flops, bytes_accessed=nbytes, transcendentals=0),
        **kwargs,
    )


def hbm(x):
    return pltpu.with_memory_space_constraint(x, pltpu.HBM)


def whole(*shape):
    return pl.BlockSpec(shape, lambda *_: (0,) * len(shape))


def embed_kernel(
    img_ref, x_hbm, w_hbm, gain_hbm, pairs_hbm, normed_hbm, pieces_hbm,
    x_scr, w_scr, gain_scr, pairs_scr, normed_scr, pieces_scr, scratch, in_sems, normed_sems, piece_sems,
):
    chunks, rows, _ = x_scr.shape
    width = w_scr.shape[1]
    per_half = width // 256
    toks = pieces_scr.shape[0] // 2
    pitch = toks + 8
    images = scratch.shape[1] // pitch
    small = [
        pltpu.make_async_copy(pairs_hbm, pairs_scr, in_sems.at[chunks + 1]),
        pltpu.make_async_copy(gain_hbm, gain_scr, in_sems.at[chunks + 2]),
    ]
    loads = [pltpu.make_async_copy(w_hbm, w_scr, in_sems.at[chunks])]
    for i in range(chunks):
        loads.append(pltpu.make_async_copy(x_hbm.at[pl.ds(i * rows, rows)], x_scr.at[i], in_sems.at[i]))
    for load in loads + small:
        load.start()
    for load in small:
        load.wait()
    gain = gain_scr[...].reshape(1, width)
    second = pairs_scr[1:2, :]
    owner = lax.div(second, images)
    numbers = jnp.concatenate([owner, second - owner * images], axis=0).astype(F32)
    count = numbers.shape[1]
    numbers = jnp.concatenate([numbers, jnp.zeros((6, count), F32)], axis=0)
    numbers = jnp.concatenate([numbers] * (128 // count), axis=1)
    place = lax.div(lax.broadcasted_iota(jnp.int32, numbers.shape, 1), count)
    numbers = jnp.where(place == lax.rem(img_ref[0], 128 // count), numbers, 0.0).astype(BF16)
    for m in range(2 * toks):
        pieces_scr[m, per_half * images:, :] = numbers
    loads[0].wait()

    def normed_out(i):
        at = pl.ds(pl.multiple_of(i * rows, rows), rows)
        return pltpu.make_async_copy(normed_scr.at[at], normed_hbm.at[at], normed_sems.at[i])

    @pl.loop(0, chunks)
    def _(i):
        at = pl.ds(pl.multiple_of(i * rows, rows), rows)
        pltpu.make_async_copy(x_hbm.at[at], x_scr.at[i], in_sems.at[i]).wait()
        e = jnp.dot(x_scr[i], w_scr[...], preferred_element_type=F32)
        c = e - jnp.mean(e, axis=-1, keepdims=True)
        spread = jnp.mean(c * c, axis=-1, keepdims=True)
        n = c * lax.rsqrt(spread + 1e-06) * gain
        normed_scr[at, :] = n.astype(BF16)
        normed_out(i).start()
        for u in range(rows // toks):
            to = pl.ds(pl.multiple_of((i * (rows // toks) + u) * pitch, 8), toks)
            for b in range(width // 128):
                scratch[b, to, :] = n[u * toks:(u + 1) * toks, b * 128:(b + 1) * 128]

    group = 8

    def outgoing(h, g):
        at = pl.ds(pl.multiple_of(h * toks + g * group, group), group)
        sem = piece_sems.at[h * (toks // group) + g]
        return pltpu.make_async_copy(pieces_scr.at[at], pieces_hbm.at[at], sem)

    @pl.loop(0, toks // group)
    def _(g):
        for h in range(2):
            for u in range(group):
                r = g * group + u
                for b in range(per_half):
                    v = scratch[h * per_half + b, pl.ds(r, images, stride=pitch), :]
                    pieces_scr[h * toks + r, b * images:(b + 1) * images, :] = v.astype(BF16)
            outgoing(h, g).start()

    @pl.loop(0, toks // group)
    def _(g):
        for h in range(2):
            outgoing(h, g).wait()

    @pl.loop(0, chunks)
    def _(i):
        normed_out(i).wait()


def gather_kernel(first_ref, tok_ref, normed_ref, f0, f1, f2, f3):
    group = tok_ref[0]
    for k, f in enumerate((f0, f1, f2, f3)):
        items, toks, _ = f.shape
        for j in range(items):
            p = first_ref[lax.rem(group + k, 4) * items + j]
            f[j] = normed_ref[pl.ds(pl.multiple_of(p * toks, toks), toks), :]


def pick_kernel(table_ref, out_ref, ids_ref):
    step = pl.program_id(0)
    owners, height, _ = table_ref.shape
    rows, half = out_ref.shape
    blocks = half // 128
    images = (height - 8) // blocks

    table = [table_ref[:, b * images:(b + 1) * images, :].reshape(owners * images, 128) for b in range(blocks)]
    table = jnp.concatenate(table, axis=1)
    image = lax.broadcasted_iota(jnp.int32, (owners * images, 128), 0).astype(F32)
    hot = []
    for q in range(rows // 128):
        wanted = jnp.zeros((1, 128), F32)
        for o in range(128 // images):
            top = table_ref[step * (rows // images) + q * (128 // images) + o, blocks * images:, :].astype(F32)
            wanted = wanted + top[0:1, :] * float(images) + top[1:2, :]
        ids_ref[q] = wanted
        hot.append(jnp.where(wanted == image, 1.0, 0.0).astype(BF16))
    hot = jnp.concatenate(hot, axis=1)
    picked = lax.dot_general(table, hot, (((0,), (0,)), ((), ())), preferred_element_type=F32)
    out_ref[...] = picked.T.astype(BF16)


def sum_kernel(ids_ref, rows_ref, out_ref):
    step = pl.program_id(0)
    images, half = out_ref.shape

    ids = ids_ref[...]
    lane = lax.broadcasted_iota(jnp.int32, ids.shape, 1) + step * images
    hot = [jnp.where(ids == lane + b * 128, 1.0, 0.0).astype(BF16) for b in range(images // 128)]
    hot = jnp.concatenate(hot, axis=1)
    total = lax.dot_general(rows_ref[...], hot, (((0,), (0,)), ((), ())), preferred_element_type=F32)
    out_ref[...] = total.T.astype(BF16)


def first_kernel(f0, f1, f2, f3, wq_ref, wkv_ref, q_ref, kv_ref):
    for k, f in enumerate((f0, f1, f2, f3)):
        items, toks, width = f.shape
        x = f[...].reshape(items * toks, width)
        q = jnp.dot(x, wq_ref[...], preferred_element_type=F32).astype(BF16)
        q_ref[:, k * toks:(k + 1) * toks, :] = q.reshape(items, toks, -1)
        kv = jnp.dot(x, wkv_ref[...], preferred_element_type=F32).astype(BF16)
        kv_ref[:, k * toks:(k + 1) * toks, :] = kv.reshape(items, toks, -1)


def masks(rows):
    lane = lax.broadcasted_iota(jnp.int32, (rows, 128), 1)
    low = lane < HEAD
    one_low = jnp.where(low, 1.0, 0.0).astype(BF16)
    one_high = jnp.where(low, 0.0, 1.0).astype(BF16)
    return low, one_low, one_high


def attend(q, k, v, low, one_low, one_high):
    rows = k.shape[0]
    zero = jnp.zeros((rows, 128), BF16)
    kk = jnp.concatenate([jnp.where(low, k, zero), jnp.where(low, zero, k)], axis=0)
    top = jnp.concatenate([jnp.where(low, v, zero), one_low], axis=1)
    bottom = jnp.concatenate([jnp.where(low, zero, v), one_high], axis=1)
    vv = jnp.concatenate([top, bottom], axis=0)
    s = lax.dot_general(q, kk, (((1,), (1,)), ((), ())), preferred_element_type=F32)
    s = s * (1.0 / HEAD ** 0.5)
    parts = []
    for part in (s[:, :rows], s[:, rows:]):
        parts.append(jnp.exp(part - jnp.max(part, axis=-1, keepdims=True)).astype(BF16))
    o = jnp.dot(jnp.concatenate(parts, axis=1), vv, preferred_element_type=F32)
    return o[:, :128] / o[:, 128:]


def by_pair(x_ref, scratch, x_scr, items):
    per_half = scratch.shape[0] // 2
    toks = scratch.shape[1] // items
    for b in range(scratch.shape[0]):
        h, at = divmod(b, per_half)
        scratch[b] = x_ref[h, :, at * 128:(at + 1) * 128].astype(F32)
        for j in range(items):
            rows = scratch[b, pl.ds(j, toks, stride=items), :]
            x_scr[j * toks:(j + 1) * toks, b * 128:(b + 1) * 128] = rows.astype(BF16)


def second_kernel(x_ref, kv_ref, wq_ref, back_ref, q_scr, o_scr):
    step = pl.program_id(0)
    steps = pl.num_programs(0)
    lane_blocks, rows, _ = q_scr.shape
    per_half = lane_blocks // 2
    per_step, toks, _ = kv_ref.shape
    width = lane_blocks * 128
    items = rows // toks

    @pl.when(step == 0)
    def _():
        for i in range(rows // 256):
            at = slice(i * 256, (i + 1) * 256)
            x = jnp.concatenate([x_ref[0, at, :], x_ref[1, at, :]], axis=1)
            q = jnp.dot(x, wq_ref[...], preferred_element_type=F32)
            for b in range(lane_blocks):
                q_scr[b, at, :] = q[:, b * 128:(b + 1) * 128]

    masked = masks(toks)
    for p in range(per_step):
        mine = pl.ds(step * per_step + p, toks, stride=items)
        for h in range(lane_blocks):
            k = kv_ref[p, :, h * 128:(h + 1) * 128]
            v = kv_ref[p, :, width + h * 128:width + (h + 1) * 128]
            o_scr[h, mine, :] = attend(q_scr[h, mine, :].astype(BF16), k, v, *masked)

    @pl.when(step == steps - 1)
    def _():
        for b in range(lane_blocks):
            h, at = divmod(b, per_half)
            back_ref[h, :, at * 128:(at + 1) * 128] = o_scr[b].astype(BF16)


def near_kernel(x_ref, q_ref, wkv_ref, g0, g1, g2, g3, scratch, x_scr, kv_scr):
    step = pl.program_id(0)
    lane_blocks = scratch.shape[0]
    rows = scratch.shape[1]
    toks = q_ref.shape[1]
    width = lane_blocks * 128

    @pl.when(step == 0)
    def _():
        by_pair(x_ref, scratch, x_scr, rows // toks)

        @pl.loop(0, rows // 256)
        def _(i):
            at = pl.ds(pl.multiple_of(i * 256, 256), 256)
            kv_scr[at, :] = jnp.dot(x_scr[at, :], wkv_ref[...], preferred_element_type=F32).astype(BF16)

    mine = pl.ds(pl.multiple_of(step * toks, toks), toks)
    masked = masks(toks)
    part = toks // 4
    for h in range(lane_blocks):
        at = slice(h * 128, (h + 1) * 128)
        v = kv_scr[mine, width + h * 128:width + (h + 1) * 128]
        o = attend(q_ref[0, :, at], kv_scr[mine, at], v, *masked).astype(BF16)
        for k, g in enumerate((g0, g1, g2, g3)):
            g[0, :, at] = o[k * part:(k + 1) * part]


def base_kernel(first_ref, tok_ref, recip_ref, normed_ref, r0, r1, r2, r3, out_ref):
    images, toks, _ = out_ref.shape
    out_ref[...] = jnp.zeros_like(out_ref)
    group = tok_ref[0]
    for k, r in enumerate((r0, r1, r2, r3)):
        items = r.shape[0]

        @pl.loop(0, items)
        def _(j, r=r, k=k, items=items):
            p = first_ref[lax.rem(group + k, 4) * items + j]
            out_ref[p] = out_ref[p] + r[j].astype(F32)

    @pl.loop(0, images)
    def _(i):
        at = pl.ds(pl.multiple_of(i * toks, toks), toks)
        out_ref[i] = out_ref[i] * recip_ref[i] + normed_ref[at, :].astype(F32)


def join_kernel(recip_ref, far_ref, base_ref, out_hbm, out_scr, scratch, sems):
    images, toks, width = base_ref.shape
    half = width // 2
    lane_blocks = width // 128
    pitch = toks + 8
    group = scratch.shape[1] // pitch
    stores = []
    for g in range(images // group):
        for b in range(lane_blocks):
            h, at = divmod(b * 128, half)
            for r in range(toks):
                far = far_ref[h * toks + r, g * group:(g + 1) * group, at:at + 128]
                scratch[b, pl.ds(r, group, stride=pitch), :] = far.astype(F32)
        for u in range(group):
            i = g * group + u
            recip = recip_ref[i]
            for b in range(lane_blocks):
                lanes = slice(b * 128, (b + 1) * 128)
                far = scratch[b, u * pitch:u * pitch + toks, :]
                out_scr[i, :, lanes] = (far * recip + base_ref[i, :, lanes]).astype(BF16)
            if u % 8 == 7:
                at = pl.ds(i - 7, 8)
                stores.append(pltpu.make_async_copy(out_scr.at[at], out_hbm.at[at], sems.at[i // 8]))
                stores[-1].start()
    for store in stores:
        store.wait()


def body(tokens, embed, norm_gain, pairs, wq_first, wkv_first, wq_second, wkv_second):
    images, toks, enc = tokens.shape
    width = embed.shape[1]
    half = width // 2
    owners = lax.axis_size("img")
    groups = lax.axis_size("tok")
    count = pairs.shape[0]
    items = count // groups
    total = owners * count
    all_images = owners * images
    rows = images * toks
    img = lax.axis_index("img")
    tok = lax.axis_index("tok").astype(jnp.int32).reshape(1)
    smem = pl.BlockSpec(memory_space=pltpu.SMEM)
    vmem = pl.BlockSpec(memory_space=pltpu.VMEM)

    first_local = pairs[:, 0] - img * images
    part = jax.ShapeDtypeStruct((items, toks, width), BF16)
    block = 256
    height = images * half // 128 + 8
    anywhere = pl.BlockSpec(memory_space=pl.ANY)
    normed, pieces = call(
        embed_kernel,
        [
            pltpu.HBM((rows, width), BF16),
            pltpu.HBM((owners, height, 128), BF16),
        ],
        2 * rows * enc * width,
        2 * rows * (enc + 2 * width) + 2 * enc * width,
        28,
        in_specs=[smem] + [anywhere] * 4,
        out_specs=[anywhere, anywhere],
        scratch_shapes=[
            pltpu.VMEM((rows // block, block, enc), BF16),
            pltpu.VMEM((enc, width), BF16),
            pltpu.VMEM((width,), F32),
            pltpu.VMEM((2, count), jnp.int32),
            pltpu.VMEM((rows, width), BF16),
            pltpu.VMEM((owners, height, 128), BF16),
            pltpu.VMEM((width // 128, images * (toks + 8), 128), F32),
            pltpu.SemaphoreType.DMA((rows // block + 3,)),
            pltpu.SemaphoreType.DMA((rows // block,)),
            pltpu.SemaphoreType.DMA((owners // 8,)),
        ],
        name="embed",
    )(img.astype(jnp.int32).reshape(1), hbm(tokens.reshape(rows, enc)), hbm(embed), hbm(norm_gain), hbm(pairs.T))

    table = lax.all_to_all(pieces, "img", split_axis=0, concat_axis=0, tiled=True)

    firsts = list(call(
        gather_kernel,
        [part] * 4,
        rows * width,
        4 * rows * width,
        8,
        in_specs=[smem, smem, vmem],
        out_specs=[vmem] * 4,
        name="gather",
    )(first_local, tok, normed))
    for k in range(1, groups):
        perm = [(t, (t + k) % groups) for t in range(groups)]
        firsts[k] = lax.ppermute(firsts[k], "tok", perm)
    table, *firsts = lax.optimization_barrier((table, *firsts))

    step_rows = 1024
    asked, ids = call(
        pick_kernel,
        [
            pltpu.HBM((total, half), BF16),
            jax.ShapeDtypeStruct((total // 128, 1, 128), F32),
        ],
        2 * total * all_images * half,
        2 * (total + all_images) * half,
        24,
        grid=(total // step_rows,),
        in_specs=[vmem],
        out_specs=[
            pl.BlockSpec((step_rows, half), lambda i: (i, 0)),
            pl.BlockSpec((step_rows // 128, 1, 128), lambda i: (i, 0, 0)),
        ],
        name="pick",
    )(table)
    ids = ids.astype(jnp.int32).reshape(total)
    seconds = lax.all_to_all(
        asked.reshape(owners * groups, items, half), ("img", "tok"), split_axis=0, concat_axis=0, tiled=True
    )

    whole_toks = toks * groups
    pair_rows = items * whole_toks
    q_first, kv_second = call(
        first_kernel,
        [
            jax.ShapeDtypeStruct((items, whole_toks, width), BF16),
            jax.ShapeDtypeStruct((items, whole_toks, 2 * width), BF16),
        ],
        2 * pair_rows * width * 3 * width,
        2 * pair_rows * width * 4 + 6 * width * width,
        20,
        in_specs=[vmem] * 6,
        out_specs=[vmem] * 2,
        name="first",
    )(*firsts, wq_first, wkv_second)
    own_ids = img * images + jnp.arange(images)
    seen = jnp.sum((ids[None, :] == own_ids[:, None]).astype(F32), axis=1)
    seen = seen + jnp.sum((pairs[:, 0][None, :] == own_ids[:, None]).astype(F32), axis=1)
    recip = 1.0 / jnp.maximum(seen, 1.0)

    seconds = seconds.reshape(2, pair_rows, half)
    back = call(
        second_kernel,
        pltpu.HBM((2, pair_rows, half), BF16),
        2 * pair_rows * width * width + 8 * pair_rows * whole_toks * width,
        2 * pair_rows * width * 4 + 2 * width * width,
        28,
        grid=(items // 2,),
        in_specs=[
            vmem,
            pl.BlockSpec((2, whole_toks, 2 * width), lambda j: (j, 0, 0)),
            vmem,
        ],
        out_specs=whole(2, pair_rows, half),
        scratch_shapes=[
            pltpu.VMEM((width // 128, pair_rows, 128), F32),
            pltpu.VMEM((width // 128, pair_rows, 128), F32),
        ],
        name="second",
    )(seconds, hbm(kv_second), wq_second)
    returned = lax.all_to_all(
        back.reshape(owners * groups, items, half), ("img", "tok"), split_axis=0, concat_axis=0, tiled=True
    )

    seconds, _ = lax.optimization_barrier((seconds, back))
    near = list(call(
        near_kernel,
        [part] * 4,
        4 * pair_rows * width * width + 8 * pair_rows * whole_toks * width,
        2 * pair_rows * width * 3 + 4 * width * width,
        28,
        grid=(items,),
        in_specs=[
            vmem,
            pl.BlockSpec((1, whole_toks, width), lambda j: (j, 0, 0)),
            vmem,
        ],
        out_specs=[pl.BlockSpec((1, toks, width), lambda j: (j, 0, 0))] * 4,
        scratch_shapes=[
            pltpu.VMEM((width // 128, pair_rows, 128), F32),
            pltpu.VMEM((pair_rows, width), BF16),
            pltpu.VMEM((pair_rows, 2 * width), BF16),
        ],
        name="near",
    )(seconds, q_first, wkv_first))
    returned, *near = lax.optimization_barrier((returned, *near))
    for k in range(1, groups):
        perm = [(t, (t - k) % groups) for t in range(groups)]
        near[k] = lax.ppermute(near[k], "tok", perm)

    sums = call(
        sum_kernel,
        pltpu.HBM((all_images, half), BF16),
        2 * total * all_images * half,
        2 * (total + all_images) * half,
        20,
        grid=(all_images // step_rows,),
        in_specs=[vmem, vmem],
        out_specs=pl.BlockSpec((step_rows, half), lambda i: (i, 0)),
        name="sum",
    )(jnp.broadcast_to(ids[:, None], (total, 128)), returned.reshape(total, half))
    far = lax.all_to_all(
        sums.reshape(owners, images, half), "img", split_axis=0, concat_axis=0, tiled=True
    )
    base = call(
        base_kernel,
        jax.ShapeDtypeStruct((images, toks, width), F32),
        rows * width,
        8 * rows * width,
        12,
        in_specs=[smem, smem, smem] + [vmem] * 5,
        out_specs=vmem,
        name="base",
    )(first_local, tok, recip, normed, *near)
    return call(
        join_kernel,
        pltpu.HBM((images, toks, width), BF16),
        rows * width * 4,
        rows * width * 8,
        24,
        in_specs=[smem, vmem, vmem],
        out_specs=anywhere,
        scratch_shapes=[
            pltpu.VMEM((images, toks, width), BF16),
            pltpu.VMEM((width // 128, images // 2 * (toks + 8), 128), F32),
            pltpu.SemaphoreType.DMA((images // 8,)),
        ],
        name="join",
    )(recip, far, base)


def solution(mesh):
    in_specs = (P("img", "tok", None), P(), P(), P("img", None), P(), P(), P(), P())
    out_specs = P("img", "tok", None)
    return jax.shard_map(body, mesh=mesh, in_specs=in_specs, out_specs=out_specs, check_vma=False)
```

```python
import jax
import jax.numpy as jnp
from jax import lax
from jax.experimental import pallas as pl
from jax.experimental.pallas import tpu as pltpu
from jax.sharding import PartitionSpec as P

HEAD = 64
MIB = 1024 * 1024
F32 = jnp.float32
BF16 = jnp.bfloat16


def call(kernel, out_shape, flops, nbytes, vmem_mib, **kwargs):
    return pl.pallas_call(
        kernel,
        out_shape=out_shape,
        compiler_params=pltpu.CompilerParams(vmem_limit_bytes=vmem_mib * MIB),
        cost_estimate=pl.CostEstimate(flops=flops, bytes_accessed=nbytes, transcendentals=0),
        **kwargs,
    )


def hbm(x):
    return pltpu.with_memory_space_constraint(x, pltpu.HBM)


def whole(*shape):
    return pl.BlockSpec(shape, lambda *_: (0,) * len(shape))


def embed_kernel(
    img_ref, x_hbm, w_hbm, gain_hbm, pairs_hbm, normed_hbm, pieces_hbm,
    x_scr, w_scr, gain_scr, pairs_scr, normed_scr, pieces_scr, scratch, in_sems, normed_sems, piece_sems,
):
    chunks, rows, _ = x_scr.shape
    width = w_scr.shape[1]
    per_half = width // 256
    toks = pieces_scr.shape[0] // 2
    pitch = toks + 8
    images = scratch.shape[1] // pitch
    small = [
        pltpu.make_async_copy(pairs_hbm, pairs_scr, in_sems.at[chunks + 1]),
        pltpu.make_async_copy(gain_hbm, gain_scr, in_sems.at[chunks + 2]),
    ]
    loads = [pltpu.make_async_copy(w_hbm, w_scr, in_sems.at[chunks])]
    for i in range(chunks):
        loads.append(pltpu.make_async_copy(x_hbm.at[pl.ds(i * rows, rows)], x_scr.at[i], in_sems.at[i]))
    for load in loads + small:
        load.start()
    for load in small:
        load.wait()
    gain = gain_scr[...].reshape(1, width)
    second = pairs_scr[1:2, :]
    owner = lax.div(second, images)
    numbers = jnp.concatenate([owner, second - owner * images], axis=0).astype(F32)
    count = numbers.shape[1]
    numbers = jnp.concatenate([numbers, jnp.zeros((6, count), F32)], axis=0)
    numbers = jnp.concatenate([numbers] * (128 // count), axis=1)
    place = lax.div(lax.broadcasted_iota(jnp.int32, numbers.shape, 1), count)
    numbers = jnp.where(place == lax.rem(img_ref[0], 128 // count), numbers, 0.0).astype(BF16)
    for m in range(2 * toks):
        pieces_scr[m, per_half * images:, :] = numbers
    loads[0].wait()

    def normed_out(i):
        at = pl.ds(pl.multiple_of(i * rows, rows), rows)
        return pltpu.make_async_copy(normed_scr.at[at], normed_hbm.at[at], normed_sems.at[i])

    @pl.loop(0, chunks)
    def _(i):
        at = pl.ds(pl.multiple_of(i * rows, rows), rows)
        pltpu.make_async_copy(x_hbm.at[at], x_scr.at[i], in_sems.at[i]).wait()
        e = jnp.dot(x_scr[i], w_scr[...], preferred_element_type=F32)
        c = e - jnp.mean(e, axis=-1, keepdims=True)
        spread = jnp.mean(c * c, axis=-1, keepdims=True)
        n = c * lax.rsqrt(spread + 1e-06) * gain
        normed_scr[at, :] = n.astype(BF16)
        normed_out(i).start()
        for u in range(rows // toks):
            to = pl.ds(pl.multiple_of((i * (rows // toks) + u) * pitch, 8), toks)
            for b in range(width // 128):
                scratch[b, to, :] = n[u * toks:(u + 1) * toks, b * 128:(b + 1) * 128]

    group = 8

    def outgoing(h, g):
        at = pl.ds(pl.multiple_of(h * toks + g * group, group), group)
        sem = piece_sems.at[h * (toks // group) + g]
        return pltpu.make_async_copy(pieces_scr.at[at], pieces_hbm.at[at], sem)

    @pl.loop(0, toks // group)
    def _(g):
        for h in range(2):
            for u in range(group):
                r = g * group + u
                for b in range(per_half):
                    v = scratch[h * per_half + b, pl.ds(r, images, stride=pitch), :]
                    pieces_scr[h * toks + r, b * images:(b + 1) * images, :] = v.astype(BF16)
            outgoing(h, g).start()

    @pl.loop(0, toks // group)
    def _(g):
        for h in range(2):
            outgoing(h, g).wait()

    @pl.loop(0, chunks)
    def _(i):
        normed_out(i).wait()


def gather_kernel(first_ref, tok_ref, normed_ref, f0, f1, f2, f3):
    group = tok_ref[0]
    for k, f in enumerate((f0, f1, f2, f3)):
        items, toks, _ = f.shape
        for j in range(items):
            p = first_ref[lax.rem(group + k, 4) * items + j]
            f[j] = normed_ref[pl.ds(pl.multiple_of(p * toks, toks), toks), :]


def pick_kernel(table_ref, out_ref, ids_ref):
    step = pl.program_id(0)
    owners, height, _ = table_ref.shape
    rows, half = out_ref.shape
    blocks = half // 128
    images = (height - 8) // blocks

    table = [table_ref[:, b * images:(b + 1) * images, :].reshape(owners * images, 128) for b in range(blocks)]
    table = jnp.concatenate(table, axis=1)
    image = lax.broadcasted_iota(jnp.int32, (owners * images, 128), 0).astype(F32)
    hot = []
    for q in range(rows // 128):
        wanted = jnp.zeros((1, 128), F32)
        for o in range(128 // images):
            top = table_ref[step * (rows // images) + q * (128 // images) + o, blocks * images:, :].astype(F32)
            wanted = wanted + top[0:1, :] * float(images) + top[1:2, :]
        ids_ref[q] = wanted
        hot.append(jnp.where(wanted == image, 1.0, 0.0).astype(BF16))
    hot = jnp.concatenate(hot, axis=1)
    picked = lax.dot_general(table, hot, (((0,), (0,)), ((), ())), preferred_element_type=F32)
    out_ref[...] = picked.T.astype(BF16)


def sum_kernel(ids_ref, rows_ref, out_ref):
    step = pl.program_id(0)
    images, half = out_ref.shape

    ids = ids_ref[...]
    lane = lax.broadcasted_iota(jnp.int32, ids.shape, 1) + step * images
    hot = [jnp.where(ids == lane + b * 128, 1.0, 0.0).astype(BF16) for b in range(images // 128)]
    hot = jnp.concatenate(hot, axis=1)
    total = lax.dot_general(rows_ref[...], hot, (((0,), (0,)), ((), ())), preferred_element_type=F32)
    out_ref[...] = total.T.astype(BF16)


def first_kernel(f0, f1, f2, f3, wq_ref, wkv_ref, q_ref, kv_ref):
    for k, f in enumerate((f0, f1, f2, f3)):
        items, toks, width = f.shape
        x = f[...].reshape(items * toks, width)
        q = jnp.dot(x, wq_ref[...], preferred_element_type=F32).astype(BF16)
        q_ref[:, k * toks:(k + 1) * toks, :] = q.reshape(items, toks, -1)
        kv = jnp.dot(x, wkv_ref[...], preferred_element_type=F32).astype(BF16)
        kv_ref[:, k * toks:(k + 1) * toks, :] = kv.reshape(items, toks, -1)


def masks(rows):
    lane = lax.broadcasted_iota(jnp.int32, (rows, 128), 1)
    low = lane < HEAD
    one_low = jnp.where(low, 1.0, 0.0).astype(BF16)
    one_high = jnp.where(low, 0.0, 1.0).astype(BF16)
    return low, one_low, one_high


def attend(q, k, v, low, one_low, one_high):
    rows = k.shape[0]
    zero = jnp.zeros((rows, 128), BF16)
    kk = jnp.concatenate([jnp.where(low, k, zero), jnp.where(low, zero, k)], axis=0)
    top = jnp.concatenate([jnp.where(low, v, zero), one_low], axis=1)
    bottom = jnp.concatenate([jnp.where(low, zero, v), one_high], axis=1)
    vv = jnp.concatenate([top, bottom], axis=0)
    s = lax.dot_general(q, kk, (((1,), (1,)), ((), ())), preferred_element_type=F32)
    s = s * (1.0 / HEAD ** 0.5)
    parts = []
    for part in (s[:, :rows], s[:, rows:]):
        parts.append(jnp.exp(part - jnp.max(part, axis=-1, keepdims=True)).astype(BF16))
    o = jnp.dot(jnp.concatenate(parts, axis=1), vv, preferred_element_type=F32)
    return o[:, :128] / o[:, 128:]


def by_pair(x_ref, scratch, x_scr, items):
    per_half = scratch.shape[0] // 2
    toks = scratch.shape[1] // items
    for b in range(scratch.shape[0]):
        h, at = divmod(b, per_half)
        scratch[b] = x_ref[h, :, at * 128:(at + 1) * 128].astype(F32)
        for j in range(items):
            rows = scratch[b, pl.ds(j, toks, stride=items), :]
            x_scr[j * toks:(j + 1) * toks, b * 128:(b + 1) * 128] = rows.astype(BF16)


def second_kernel(x_ref, kv_ref, wq_ref, back_hbm, q_scr, o_scr, back_scr, sems):
    step = pl.program_id(0)
    steps = pl.num_programs(0)
    lane_blocks, rows, _ = q_scr.shape
    per_half = lane_blocks // 2
    per_step, toks, _ = kv_ref.shape
    width = lane_blocks * 128
    items = rows // toks

    @pl.when(step == 0)
    def _():
        for i in range(rows // 256):
            at = slice(i * 256, (i + 1) * 256)
            x = jnp.concatenate([x_ref[0, at, :], x_ref[1, at, :]], axis=1)
            q = jnp.dot(x, wq_ref[...], preferred_element_type=F32)
            for b in range(lane_blocks):
                q_scr[b, at, :] = q[:, b * 128:(b + 1) * 128]

    masked = masks(toks)
    for p in range(per_step):
        mine = pl.ds(step * per_step + p, toks, stride=items)
        for h in range(lane_blocks):
            k = kv_ref[p, :, h * 128:(h + 1) * 128]
            v = kv_ref[p, :, width + h * 128:width + (h + 1) * 128]
            o_scr[h, mine, :] = attend(q_scr[h, mine, :].astype(BF16), k, v, *masked)

    @pl.when(step == steps - 1)
    def _():
        stores = []
        for h in range(2):
            for q in range(2):
                rows_at = pl.ds(q * (rows // 2), rows // 2)
                for at in range(per_half):
                    piece = o_scr[h * per_half + at, rows_at, :].astype(BF16)
                    back_scr[h, rows_at, at * 128:(at + 1) * 128] = piece
                sem = sems.at[h * 2 + q]
                stores.append(pltpu.make_async_copy(back_scr.at[h, rows_at], back_hbm.at[h, rows_at], sem))
                stores[-1].start()
        for store in stores:
            store.wait()


def near_kernel(x_ref, q_ref, wkv_ref, g0, g1, g2, g3, scratch, x_scr, kv_scr):
    step = pl.program_id(0)
    lane_blocks = scratch.shape[0]
    rows = scratch.shape[1]
    toks = q_ref.shape[1]
    width = lane_blocks * 128

    @pl.when(step == 0)
    def _():
        by_pair(x_ref, scratch, x_scr, rows // toks)

        @pl.loop(0, rows // 256)
        def _(i):
            at = pl.ds(pl.multiple_of(i * 256, 256), 256)
            kv_scr[at, :] = jnp.dot(x_scr[at, :], wkv_ref[...], preferred_element_type=F32).astype(BF16)

    mine = pl.ds(pl.multiple_of(step * toks, toks), toks)
    masked = masks(toks)
    part = toks // 4
    for h in range(lane_blocks):
        at = slice(h * 128, (h + 1) * 128)
        v = kv_scr[mine, width + h * 128:width + (h + 1) * 128]
        o = attend(q_ref[0, :, at], kv_scr[mine, at], v, *masked).astype(BF16)
        for k, g in enumerate((g0, g1, g2, g3)):
            g[0, :, at] = o[k * part:(k + 1) * part]


def base_kernel(first_ref, tok_ref, recip_ref, normed_ref, r0, r1, r2, r3, out_ref):
    images, toks, _ = out_ref.shape
    out_ref[...] = jnp.zeros_like(out_ref)
    group = tok_ref[0]
    for k, r in enumerate((r0, r1, r2, r3)):
        items = r.shape[0]

        @pl.loop(0, items)
        def _(j, r=r, k=k, items=items):
            p = first_ref[lax.rem(group + k, 4) * items + j]
            out_ref[p] = out_ref[p] + r[j].astype(F32)

    @pl.loop(0, images)
    def _(i):
        at = pl.ds(pl.multiple_of(i * toks, toks), toks)
        out_ref[i] = out_ref[i] * recip_ref[i] + normed_ref[at, :].astype(F32)


def join_kernel(recip_ref, far_ref, base_ref, out_hbm, out_scr, scratch, sems):
    images, toks, width = base_ref.shape
    half = width // 2
    lane_blocks = width // 128
    pitch = toks + 8
    group = scratch.shape[1] // pitch
    stores = []
    for g in range(images // group):
        for b in range(lane_blocks):
            h, at = divmod(b * 128, half)
            for r in range(toks):
                far = far_ref[h * toks + r, g * group:(g + 1) * group, at:at + 128]
                scratch[b, pl.ds(r, group, stride=pitch), :] = far.astype(F32)
        for u in range(group):
            i = g * group + u
            recip = recip_ref[i]
            for b in range(lane_blocks):
                lanes = slice(b * 128, (b + 1) * 128)
                far = scratch[b, u * pitch:u * pitch + toks, :]
                out_scr[i, :, lanes] = (far * recip + base_ref[i, :, lanes]).astype(BF16)
            if u % 8 == 7:
                at = pl.ds(i - 7, 8)
                stores.append(pltpu.make_async_copy(out_scr.at[at], out_hbm.at[at], sems.at[i // 8]))
                stores[-1].start()
    for store in stores:
        store.wait()


def body(tokens, embed, norm_gain, pairs, wq_first, wkv_first, wq_second, wkv_second):
    images, toks, enc = tokens.shape
    width = embed.shape[1]
    half = width // 2
    owners = lax.axis_size("img")
    groups = lax.axis_size("tok")
    count = pairs.shape[0]
    items = count // groups
    total = owners * count
    all_images = owners * images
    rows = images * toks
    img = lax.axis_index("img")
    tok = lax.axis_index("tok").astype(jnp.int32).reshape(1)
    smem = pl.BlockSpec(memory_space=pltpu.SMEM)
    vmem = pl.BlockSpec(memory_space=pltpu.VMEM)

    first_local = pairs[:, 0] - img * images
    part = jax.ShapeDtypeStruct((items, toks, width), BF16)
    block = 256
    height = images * half // 128 + 8
    anywhere = pl.BlockSpec(memory_space=pl.ANY)
    normed, pieces = call(
        embed_kernel,
        [
            pltpu.HBM((rows, width), BF16),
            pltpu.HBM((owners, height, 128), BF16),
        ],
        2 * rows * enc * width,
        2 * rows * (enc + 2 * width) + 2 * enc * width,
        28,
        in_specs=[smem] + [anywhere] * 4,
        out_specs=[anywhere, anywhere],
        scratch_shapes=[
            pltpu.VMEM((rows // block, block, enc), BF16),
            pltpu.VMEM((enc, width), BF16),
            pltpu.VMEM((width,), F32),
            pltpu.VMEM((2, count), jnp.int32),
            pltpu.VMEM((rows, width), BF16),
            pltpu.VMEM((owners, height, 128), BF16),
            pltpu.VMEM((width // 128, images * (toks + 8), 128), F32),
            pltpu.SemaphoreType.DMA((rows // block + 3,)),
            pltpu.SemaphoreType.DMA((rows // block,)),
            pltpu.SemaphoreType.DMA((owners // 8,)),
        ],
        name="embed",
    )(img.astype(jnp.int32).reshape(1), hbm(tokens.reshape(rows, enc)), hbm(embed), hbm(norm_gain), hbm(pairs.T))

    table = lax.all_to_all(pieces, "img", split_axis=0, concat_axis=0, tiled=True)

    firsts = list(call(
        gather_kernel,
        [part] * 4,
        rows * width,
        4 * rows * width,
        8,
        in_specs=[smem, smem, vmem],
        out_specs=[vmem] * 4,
        name="gather",
    )(first_local, tok, normed))
    for k in range(1, groups):
        perm = [(t, (t + k) % groups) for t in range(groups)]
        firsts[k] = lax.ppermute(firsts[k], "tok", perm)
    table, *firsts = lax.optimization_barrier((table, *firsts))

    step_rows = 1024
    asked, ids = call(
        pick_kernel,
        [
            pltpu.HBM((total, half), BF16),
            jax.ShapeDtypeStruct((total // 128, 1, 128), F32),
        ],
        2 * total * all_images * half,
        2 * (total + all_images) * half,
        24,
        grid=(total // step_rows,),
        in_specs=[vmem],
        out_specs=[
            pl.BlockSpec((step_rows, half), lambda i: (i, 0)),
            pl.BlockSpec((step_rows // 128, 1, 128), lambda i: (i, 0, 0)),
        ],
        name="pick",
    )(table)
    ids = ids.astype(jnp.int32).reshape(total)
    seconds = lax.all_to_all(
        asked.reshape(owners * groups, items, half), ("img", "tok"), split_axis=0, concat_axis=0, tiled=True
    )

    whole_toks = toks * groups
    pair_rows = items * whole_toks
    q_first, kv_second = call(
        first_kernel,
        [
            jax.ShapeDtypeStruct((items, whole_toks, width), BF16),
            jax.ShapeDtypeStruct((items, whole_toks, 2 * width), BF16),
        ],
        2 * pair_rows * width * 3 * width,
        2 * pair_rows * width * 4 + 6 * width * width,
        20,
        in_specs=[vmem] * 6,
        out_specs=[vmem] * 2,
        name="first",
    )(*firsts, wq_first, wkv_second)
    own_ids = img * images + jnp.arange(images)
    seen = jnp.sum((ids[None, :] == own_ids[:, None]).astype(F32), axis=1)
    seen = seen + jnp.sum((pairs[:, 0][None, :] == own_ids[:, None]).astype(F32), axis=1)
    recip = 1.0 / jnp.maximum(seen, 1.0)

    seconds = seconds.reshape(2, pair_rows, half)
    back = call(
        second_kernel,
        pltpu.HBM((2, pair_rows, half), BF16),
        2 * pair_rows * width * width + 8 * pair_rows * whole_toks * width,
        2 * pair_rows * width * 4 + 2 * width * width,
        28,
        grid=(items // 4,),
        in_specs=[
            vmem,
            pl.BlockSpec((4, whole_toks, 2 * width), lambda j: (j, 0, 0)),
            vmem,
        ],
        out_specs=anywhere,
        scratch_shapes=[
            pltpu.VMEM((width // 128, pair_rows, 128), F32),
            pltpu.VMEM((width // 128, pair_rows, 128), F32),
            pltpu.VMEM((2, pair_rows, half), BF16),
            pltpu.SemaphoreType.DMA((4,)),
        ],
        name="second",
    )(seconds, hbm(kv_second), wq_second)
    returned = lax.all_to_all(
        back.reshape(owners * groups, items, half), ("img", "tok"), split_axis=0, concat_axis=0, tiled=True
    )

    seconds, _ = lax.optimization_barrier((seconds, back))
    near = list(call(
        near_kernel,
        [part] * 4,
        4 * pair_rows * width * width + 8 * pair_rows * whole_toks * width,
        2 * pair_rows * width * 3 + 4 * width * width,
        28,
        grid=(items,),
        in_specs=[
            vmem,
            pl.BlockSpec((1, whole_toks, width), lambda j: (j, 0, 0)),
            vmem,
        ],
        out_specs=[pl.BlockSpec((1, toks, width), lambda j: (j, 0, 0))] * 4,
        scratch_shapes=[
            pltpu.VMEM((width // 128, pair_rows, 128), F32),
            pltpu.VMEM((pair_rows, width), BF16),
            pltpu.VMEM((pair_rows, 2 * width), BF16),
        ],
        name="near",
    )(seconds, q_first, wkv_first))
    returned, *near = lax.optimization_barrier((returned, *near))
    for k in range(1, groups):
        perm = [(t, (t - k) % groups) for t in range(groups)]
        near[k] = lax.ppermute(near[k], "tok", perm)

    sums = call(
        sum_kernel,
        pltpu.HBM((all_images, half), BF16),
        2 * total * all_images * half,
        2 * (total + all_images) * half,
        20,
        grid=(all_images // step_rows,),
        in_specs=[vmem, vmem],
        out_specs=pl.BlockSpec((step_rows, half), lambda i: (i, 0)),
        name="sum",
    )(jnp.broadcast_to(ids[:, None], (total, 128)), returned.reshape(total, half))
    far = lax.all_to_all(
        sums.reshape(owners, images, half), "img", split_axis=0, concat_axis=0, tiled=True
    )
    base = call(
        base_kernel,
        jax.ShapeDtypeStruct((images, toks, width), F32),
        rows * width,
        8 * rows * width,
        12,
        in_specs=[smem, smem, smem] + [vmem] * 5,
        out_specs=vmem,
        name="base",
    )(first_local, tok, recip, normed, *near)
    return call(
        join_kernel,
        pltpu.HBM((images, toks, width), BF16),
        rows * width * 4,
        rows * width * 8,
        24,
        in_specs=[smem, vmem, vmem],
        out_specs=anywhere,
        scratch_shapes=[
            pltpu.VMEM((images, toks, width), BF16),
            pltpu.VMEM((width // 128, images // 2 * (toks + 8), 128), F32),
            pltpu.SemaphoreType.DMA((images // 8,)),
        ],
        name="join",
    )(recip, far, base)


def solution(mesh):
    in_specs = (P("img", "tok", None), P(), P(), P("img", None), P(), P(), P(), P())
    out_specs = P("img", "tok", None)
    return jax.shard_map(body, mesh=mesh, in_specs=in_specs, out_specs=out_specs, check_vma=False)
```

```python
import jax
import jax.numpy as jnp
from jax import lax
from jax.experimental import pallas as pl
from jax.experimental.pallas import tpu as pltpu
from jax.sharding import PartitionSpec as P

HEAD = 64
MIB = 1024 * 1024
F32 = jnp.float32
BF16 = jnp.bfloat16


def call(kernel, out_shape, flops, nbytes, vmem_mib, **kwargs):
    return pl.pallas_call(
        kernel,
        out_shape=out_shape,
        compiler_params=pltpu.CompilerParams(vmem_limit_bytes=vmem_mib * MIB),
        cost_estimate=pl.CostEstimate(flops=flops, bytes_accessed=nbytes, transcendentals=0),
        **kwargs,
    )


def hbm(x):
    return pltpu.with_memory_space_constraint(x, pltpu.HBM)


def whole(*shape):
    return pl.BlockSpec(shape, lambda *_: (0,) * len(shape))


def embed_kernel(
    img_ref, x_hbm, w_hbm, gain_hbm, pairs_hbm, normed_hbm, pieces_hbm,
    x_scr, w_scr, gain_scr, pairs_scr, normed_scr, pieces_scr, scratch, in_sems, normed_sems, piece_sems,
):
    chunks, rows, _ = x_scr.shape
    width = w_scr.shape[1]
    per_half = width // 256
    toks = pieces_scr.shape[0] // 2
    pitch = toks + 8
    images = scratch.shape[1] // pitch
    small = [
        pltpu.make_async_copy(pairs_hbm, pairs_scr, in_sems.at[chunks + 1]),
        pltpu.make_async_copy(gain_hbm, gain_scr, in_sems.at[chunks + 2]),
    ]
    loads = [pltpu.make_async_copy(w_hbm, w_scr, in_sems.at[chunks])]
    for i in range(chunks):
        loads.append(pltpu.make_async_copy(x_hbm.at[pl.ds(i * rows, rows)], x_scr.at[i], in_sems.at[i]))
    for load in loads + small:
        load.start()
    for load in small:
        load.wait()
    gain = gain_scr[...].reshape(1, width)
    second = pairs_scr[1:2, :]
    owner = lax.div(second, images)
    numbers = jnp.concatenate([owner, second - owner * images], axis=0).astype(F32)
    count = numbers.shape[1]
    numbers = jnp.concatenate([numbers, jnp.zeros((6, count), F32)], axis=0)
    numbers = jnp.concatenate([numbers] * (128 // count), axis=1)
    place = lax.div(lax.broadcasted_iota(jnp.int32, numbers.shape, 1), count)
    numbers = jnp.where(place == lax.rem(img_ref[0], 128 // count), numbers, 0.0).astype(BF16)
    for m in range(2 * toks):
        pieces_scr[m, per_half * images:, :] = numbers
    loads[0].wait()

    def normed_out(i):
        at = pl.ds(pl.multiple_of(i * rows, rows), rows)
        return pltpu.make_async_copy(normed_scr.at[at], normed_hbm.at[at], normed_sems.at[i])

    @pl.loop(0, chunks)
    def _(i):
        at = pl.ds(pl.multiple_of(i * rows, rows), rows)
        pltpu.make_async_copy(x_hbm.at[at], x_scr.at[i], in_sems.at[i]).wait()
        e = jnp.dot(x_scr[i], w_scr[...], preferred_element_type=F32)
        c = e - jnp.mean(e, axis=-1, keepdims=True)
        spread = jnp.mean(c * c, axis=-1, keepdims=True)
        n = c * lax.rsqrt(spread + 1e-06) * gain
        normed_scr[at, :] = n.astype(BF16)
        normed_out(i).start()
        for u in range(rows // toks):
            to = pl.ds(pl.multiple_of((i * (rows // toks) + u) * pitch, 8), toks)
            for b in range(width // 128):
                scratch[b, to, :] = n[u * toks:(u + 1) * toks, b * 128:(b + 1) * 128]

    group = 8

    def outgoing(h, g):
        at = pl.ds(pl.multiple_of(h * toks + g * group, group), group)
        sem = piece_sems.at[h * (toks // group) + g]
        return pltpu.make_async_copy(pieces_scr.at[at], pieces_hbm.at[at], sem)

    @pl.loop(0, toks // group)
    def _(g):
        for h in range(2):
            for u in range(group):
                r = g * group + u
                for b in range(per_half):
                    v = scratch[h * per_half + b, pl.ds(r, images, stride=pitch), :]
                    pieces_scr[h * toks + r, b * images:(b + 1) * images, :] = v.astype(BF16)
            outgoing(h, g).start()

    @pl.loop(0, toks // group)
    def _(g):
        for h in range(2):
            outgoing(h, g).wait()

    @pl.loop(0, chunks)
    def _(i):
        normed_out(i).wait()


def gather_kernel(first_ref, tok_ref, normed_ref, f0, f1, f2, f3):
    group = tok_ref[0]
    for k, f in enumerate((f0, f1, f2, f3)):
        items, toks, _ = f.shape
        for j in range(items):
            p = first_ref[lax.rem(group + k, 4) * items + j]
            f[j] = normed_ref[pl.ds(pl.multiple_of(p * toks, toks), toks), :]


def pick_kernel(table_ref, out_ref, ids_ref):
    step = pl.program_id(0)
    owners, height, _ = table_ref.shape
    rows, half = out_ref.shape
    blocks = half // 128
    images = (height - 8) // blocks

    table = [table_ref[:, b * images:(b + 1) * images, :].reshape(owners * images, 128) for b in range(blocks)]
    table = jnp.concatenate(table, axis=1)
    image = lax.broadcasted_iota(jnp.int32, (owners * images, 128), 0).astype(F32)
    hot = []
    for q in range(rows // 128):
        wanted = jnp.zeros((1, 128), F32)
        for o in range(128 // images):
            top = table_ref[step * (rows // images) + q * (128 // images) + o, blocks * images:, :].astype(F32)
            wanted = wanted + top[0:1, :] * float(images) + top[1:2, :]
        ids_ref[q] = wanted
        hot.append(jnp.where(wanted == image, 1.0, 0.0).astype(BF16))
    hot = jnp.concatenate(hot, axis=1)
    picked = lax.dot_general(table, hot, (((0,), (0,)), ((), ())), preferred_element_type=F32)
    out_ref[...] = picked.T.astype(BF16)


def sum_kernel(ids_ref, rows_ref, out_ref):
    step = pl.program_id(0)
    images, half = out_ref.shape

    ids = ids_ref[...]
    lane = lax.broadcasted_iota(jnp.int32, ids.shape, 1) + step * images
    hot = [jnp.where(ids == lane + b * 128, 1.0, 0.0).astype(BF16) for b in range(images // 128)]
    hot = jnp.concatenate(hot, axis=1)
    total = lax.dot_general(rows_ref[...], hot, (((0,), (0,)), ((), ())), preferred_element_type=F32)
    out_ref[...] = total.T.astype(BF16)


def first_kernel(f0, f1, f2, f3, wq_ref, wkv_ref, q_ref, kv_ref):
    for k, f in enumerate((f0, f1, f2, f3)):
        items, toks, width = f.shape
        x = f[...].reshape(items * toks, width)
        q = jnp.dot(x, wq_ref[...], preferred_element_type=F32).astype(BF16)
        q_ref[:, k * toks:(k + 1) * toks, :] = q.reshape(items, toks, -1)
        kv = jnp.dot(x, wkv_ref[...], preferred_element_type=F32).astype(BF16)
        kv_ref[:, k * toks:(k + 1) * toks, :] = kv.reshape(items, toks, -1)


def masks(rows):
    lane = lax.broadcasted_iota(jnp.int32, (rows, 128), 1)
    low = lane < HEAD
    one_low = jnp.where(low, 1.0, 0.0).astype(BF16)
    one_high = jnp.where(low, 0.0, 1.0).astype(BF16)
    return low, one_low, one_high


def attend(q, k, v, low, one_low, one_high):
    rows = k.shape[0]
    zero = jnp.zeros((rows, 128), BF16)
    kk = jnp.concatenate([jnp.where(low, k, zero), jnp.where(low, zero, k)], axis=0)
    top = jnp.concatenate([jnp.where(low, v, zero), one_low], axis=1)
    bottom = jnp.concatenate([jnp.where(low, zero, v), one_high], axis=1)
    vv = jnp.concatenate([top, bottom], axis=0)
    s = lax.dot_general(q, kk, (((1,), (1,)), ((), ())), preferred_element_type=F32)
    s = s * (1.0 / HEAD ** 0.5)
    parts = []
    for part in (s[:, :rows], s[:, rows:]):
        parts.append(jnp.exp(part - jnp.max(part, axis=-1, keepdims=True)).astype(BF16))
    o = jnp.dot(jnp.concatenate(parts, axis=1), vv, preferred_element_type=F32)
    return o[:, :128] / o[:, 128:]


def by_pair(x_ref, scratch, x_scr, items):
    per_half = scratch.shape[0] // 2
    toks = scratch.shape[1] // items
    for b in range(scratch.shape[0]):
        h, at = divmod(b, per_half)
        scratch[b] = x_ref[h, :, at * 128:(at + 1) * 128].astype(F32)
        for j in range(items):
            rows = scratch[b, pl.ds(j, toks, stride=items), :]
            x_scr[j * toks:(j + 1) * toks, b * 128:(b + 1) * 128] = rows.astype(BF16)


def second_kernel(x_ref, kv_ref, wq_ref, back_hbm, q_scr, o_scr, back_scr, sems):
    step = pl.program_id(0)
    steps = pl.num_programs(0)
    lane_blocks, rows, _ = q_scr.shape
    per_half = lane_blocks // 2
    per_step, toks, _ = kv_ref.shape
    width = lane_blocks * 128
    items = rows // toks

    @pl.when(step == 0)
    def _():
        for i in range(rows // 256):
            at = slice(i * 256, (i + 1) * 256)
            x = jnp.concatenate([x_ref[0, at, :], x_ref[1, at, :]], axis=1)
            q = jnp.dot(x, wq_ref[...], preferred_element_type=F32)
            for b in range(lane_blocks):
                q_scr[b, at, :] = q[:, b * 128:(b + 1) * 128]

    masked = masks(toks)
    for p in range(per_step):
        mine = pl.ds(step * per_step + p, toks, stride=items)
        for h in range(lane_blocks):
            k = kv_ref[p, :, h * 128:(h + 1) * 128]
            v = kv_ref[p, :, width + h * 128:width + (h + 1) * 128]
            o_scr[h, mine, :] = attend(q_scr[h, mine, :].astype(BF16), k, v, *masked)

    @pl.when(step == steps - 1)
    def _():
        stores = []
        for h in range(2):
            for q in range(2):
                rows_at = pl.ds(q * (rows // 2), rows // 2)
                for at in range(per_half):
                    piece = o_scr[h * per_half + at, rows_at, :].astype(BF16)
                    back_scr[h, rows_at, at * 128:(at + 1) * 128] = piece
                sem = sems.at[h * 2 + q]
                stores.append(pltpu.make_async_copy(back_scr.at[h, rows_at], back_hbm.at[h, rows_at], sem))
                stores[-1].start()
        for store in stores:
            store.wait()


def near_kernel(x_ref, q_ref, wkv_ref, g0, g1, g2, g3, scratch, x_scr, kv_scr):
    step = pl.program_id(0)
    lane_blocks = scratch.shape[0]
    rows = scratch.shape[1]
    toks = q_ref.shape[1]
    width = lane_blocks * 128

    @pl.when(step == 0)
    def _():
        by_pair(x_ref, scratch, x_scr, rows // toks)

        @pl.loop(0, rows // 256)
        def _(i):
            at = pl.ds(pl.multiple_of(i * 256, 256), 256)
            kv_scr[at, :] = jnp.dot(x_scr[at, :], wkv_ref[...], preferred_element_type=F32).astype(BF16)

    mine = pl.ds(pl.multiple_of(step * toks, toks), toks)
    masked = masks(toks)
    part = toks // 4
    for h in range(lane_blocks):
        at = slice(h * 128, (h + 1) * 128)
        v = kv_scr[mine, width + h * 128:width + (h + 1) * 128]
        o = attend(q_ref[0, :, at], kv_scr[mine, at], v, *masked).astype(BF16)
        for k, g in enumerate((g0, g1, g2, g3)):
            g[0, :, at] = o[k * part:(k + 1) * part]


def base_kernel(first_ref, tok_ref, recip_ref, normed_ref, r0, r1, r2, r3, out_ref):
    images, toks, _ = out_ref.shape
    out_ref[...] = jnp.zeros_like(out_ref)
    group = tok_ref[0]
    for k, r in enumerate((r0, r1, r2, r3)):
        items = r.shape[0]

        @pl.loop(0, items)
        def _(j, r=r, k=k, items=items):
            p = first_ref[lax.rem(group + k, 4) * items + j]
            out_ref[p] = out_ref[p] + r[j].astype(F32)

    @pl.loop(0, images)
    def _(i):
        at = pl.ds(pl.multiple_of(i * toks, toks), toks)
        out_ref[i] = out_ref[i] * recip_ref[i] + normed_ref[at, :].astype(F32)


def join_kernel(recip_ref, far_ref, base_ref, out_hbm, out_scr, scratch, sems):
    images, toks, width = base_ref.shape
    half = width // 2
    lane_blocks = width // 128
    pitch = toks + 8
    group = scratch.shape[1] // pitch
    stores = []
    for g in range(images // group):
        for b in range(lane_blocks):
            h, at = divmod(b * 128, half)
            for r in range(toks):
                far = far_ref[h * toks + r, g * group:(g + 1) * group, at:at + 128]
                scratch[b, pl.ds(r, group, stride=pitch), :] = far.astype(F32)
        for u in range(group):
            i = g * group + u
            recip = recip_ref[i]
            for b in range(lane_blocks):
                lanes = slice(b * 128, (b + 1) * 128)
                far = scratch[b, u * pitch:u * pitch + toks, :]
                out_scr[i, :, lanes] = (far * recip + base_ref[i, :, lanes]).astype(BF16)
            if u % 8 == 7:
                at = pl.ds(i - 7, 8)
                stores.append(pltpu.make_async_copy(out_scr.at[at], out_hbm.at[at], sems.at[i // 8]))
                stores[-1].start()
    for store in stores:
        store.wait()


def body(tokens, embed, norm_gain, pairs, wq_first, wkv_first, wq_second, wkv_second):
    images, toks, enc = tokens.shape
    width = embed.shape[1]
    half = width // 2
    owners = lax.axis_size("img")
    groups = lax.axis_size("tok")
    count = pairs.shape[0]
    items = count // groups
    total = owners * count
    all_images = owners * images
    rows = images * toks
    img = lax.axis_index("img")
    tok = lax.axis_index("tok").astype(jnp.int32).reshape(1)
    smem = pl.BlockSpec(memory_space=pltpu.SMEM)
    vmem = pl.BlockSpec(memory_space=pltpu.VMEM)

    first_local = pairs[:, 0] - img * images
    part = jax.ShapeDtypeStruct((items, toks, width), BF16)
    block = 512
    height = images * half // 128 + 8
    anywhere = pl.BlockSpec(memory_space=pl.ANY)
    normed, pieces = call(
        embed_kernel,
        [
            pltpu.HBM((rows, width), BF16),
            pltpu.HBM((owners, height, 128), BF16),
        ],
        2 * rows * enc * width,
        2 * rows * (enc + 2 * width) + 2 * enc * width,
        28,
        in_specs=[smem] + [anywhere] * 4,
        out_specs=[anywhere, anywhere],
        scratch_shapes=[
            pltpu.VMEM((rows // block, block, enc), BF16),
            pltpu.VMEM((enc, width), BF16),
            pltpu.VMEM((width,), F32),
            pltpu.VMEM((2, count), jnp.int32),
            pltpu.VMEM((rows, width), BF16),
            pltpu.VMEM((owners, height, 128), BF16),
            pltpu.VMEM((width // 128, images * (toks + 8), 128), F32),
            pltpu.SemaphoreType.DMA((rows // block + 3,)),
            pltpu.SemaphoreType.DMA((rows // block,)),
            pltpu.SemaphoreType.DMA((owners // 8,)),
        ],
        name="embed",
    )(img.astype(jnp.int32).reshape(1), hbm(tokens.reshape(rows, enc)), hbm(embed), hbm(norm_gain), hbm(pairs.T))

    table = lax.all_to_all(pieces, "img", split_axis=0, concat_axis=0, tiled=True)

    firsts = list(call(
        gather_kernel,
        [part] * 4,
        rows * width,
        4 * rows * width,
        8,
        in_specs=[smem, smem, vmem],
        out_specs=[vmem] * 4,
        name="gather",
    )(first_local, tok, normed))
    for k in range(1, groups):
        perm = [(t, (t + k) % groups) for t in range(groups)]
        firsts[k] = lax.ppermute(firsts[k], "tok", perm)
    table, *firsts = lax.optimization_barrier((table, *firsts))

    step_rows = 1024
    asked, ids = call(
        pick_kernel,
        [
            pltpu.HBM((total, half), BF16),
            jax.ShapeDtypeStruct((total // 128, 1, 128), F32),
        ],
        2 * total * all_images * half,
        2 * (total + all_images) * half,
        24,
        grid=(total // step_rows,),
        in_specs=[vmem],
        out_specs=[
            pl.BlockSpec((step_rows, half), lambda i: (i, 0)),
            pl.BlockSpec((step_rows // 128, 1, 128), lambda i: (i, 0, 0)),
        ],
        name="pick",
    )(table)
    ids = ids.astype(jnp.int32).reshape(total)
    seconds = lax.all_to_all(
        asked.reshape(owners * groups, items, half), ("img", "tok"), split_axis=0, concat_axis=0, tiled=True
    )

    whole_toks = toks * groups
    pair_rows = items * whole_toks
    q_first, kv_second = call(
        first_kernel,
        [
            jax.ShapeDtypeStruct((items, whole_toks, width), BF16),
            jax.ShapeDtypeStruct((items, whole_toks, 2 * width), BF16),
        ],
        2 * pair_rows * width * 3 * width,
        2 * pair_rows * width * 4 + 6 * width * width,
        20,
        in_specs=[vmem] * 6,
        out_specs=[vmem] * 2,
        name="first",
    )(*firsts, wq_first, wkv_second)
    own_ids = img * images + jnp.arange(images)
    seen = jnp.sum((ids[None, :] == own_ids[:, None]).astype(F32), axis=1)
    seen = seen + jnp.sum((pairs[:, 0][None, :] == own_ids[:, None]).astype(F32), axis=1)
    recip = 1.0 / jnp.maximum(seen, 1.0)

    seconds = seconds.reshape(2, pair_rows, half)
    back = call(
        second_kernel,
        pltpu.HBM((2, pair_rows, half), BF16),
        2 * pair_rows * width * width + 8 * pair_rows * whole_toks * width,
        2 * pair_rows * width * 4 + 2 * width * width,
        28,
        grid=(items // 4,),
        in_specs=[
            vmem,
            pl.BlockSpec((4, whole_toks, 2 * width), lambda j: (j, 0, 0)),
            vmem,
        ],
        out_specs=anywhere,
        scratch_shapes=[
            pltpu.VMEM((width // 128, pair_rows, 128), F32),
            pltpu.VMEM((width // 128, pair_rows, 128), F32),
            pltpu.VMEM((2, pair_rows, half), BF16),
            pltpu.SemaphoreType.DMA((4,)),
        ],
        name="second",
    )(seconds, hbm(kv_second), wq_second)
    returned = lax.all_to_all(
        back.reshape(owners * groups, items, half), ("img", "tok"), split_axis=0, concat_axis=0, tiled=True
    )

    seconds, _ = lax.optimization_barrier((seconds, back))
    near = list(call(
        near_kernel,
        [part] * 4,
        4 * pair_rows * width * width + 8 * pair_rows * whole_toks * width,
        2 * pair_rows * width * 3 + 4 * width * width,
        28,
        grid=(items,),
        in_specs=[
            vmem,
            pl.BlockSpec((1, whole_toks, width), lambda j: (j, 0, 0)),
            vmem,
        ],
        out_specs=[pl.BlockSpec((1, toks, width), lambda j: (j, 0, 0))] * 4,
        scratch_shapes=[
            pltpu.VMEM((width // 128, pair_rows, 128), F32),
            pltpu.VMEM((pair_rows, width), BF16),
            pltpu.VMEM((pair_rows, 2 * width), BF16),
        ],
        name="near",
    )(seconds, q_first, wkv_first))
    returned, *near = lax.optimization_barrier((returned, *near))
    for k in range(1, groups):
        perm = [(t, (t - k) % groups) for t in range(groups)]
        near[k] = lax.ppermute(near[k], "tok", perm)

    sums = call(
        sum_kernel,
        pltpu.HBM((all_images, half), BF16),
        2 * total * all_images * half,
        2 * (total + all_images) * half,
        20,
        grid=(all_images // step_rows,),
        in_specs=[vmem, vmem],
        out_specs=pl.BlockSpec((step_rows, half), lambda i: (i, 0)),
        name="sum",
    )(jnp.broadcast_to(ids[:, None], (total, 128)), returned.reshape(total, half))
    far = lax.all_to_all(
        sums.reshape(owners, images, half), "img", split_axis=0, concat_axis=0, tiled=True
    )
    base = call(
        base_kernel,
        jax.ShapeDtypeStruct((images, toks, width), F32),
        rows * width,
        8 * rows * width,
        12,
        in_specs=[smem, smem, smem] + [vmem] * 5,
        out_specs=vmem,
        name="base",
    )(first_local, tok, recip, normed, *near)
    return call(
        join_kernel,
        pltpu.HBM((images, toks, width), BF16),
        rows * width * 4,
        rows * width * 8,
        24,
        in_specs=[smem, vmem, vmem],
        out_specs=anywhere,
        scratch_shapes=[
            pltpu.VMEM((images, toks, width), BF16),
            pltpu.VMEM((width // 128, images // 2 * (toks + 8), 128), F32),
            pltpu.SemaphoreType.DMA((images // 8,)),
        ],
        name="join",
    )(recip, far, base)


def solution(mesh):
    in_specs = (P("img", "tok", None), P(), P(), P("img", None), P(), P(), P(), P())
    out_specs = P("img", "tok", None)
    return jax.shard_map(body, mesh=mesh, in_specs=in_specs, out_specs=out_specs, check_vma=False)
```
